32 devices in a mesh: section: 2 (over core), frame: 2 (over y), tile: 8 (over z, x).
Axes of the slice: x: 2, y: 2, z: 4, core: 2. Of those that a mesh axis runs over, the one named last changes fastest.
Arguments:
- queries: bfloat16 [2, 8, 256, 1536], P('frame', 'tile', None, 'section'), may hold values from -5 to 5
- key_rows: bfloat16 [2, 8, 256, 1536], P('frame', 'tile', None, 'section'), may hold values from -5 to 5
- value_rows: bfloat16 [2, 8, 256, 1536], P('frame', 'tile', None, 'section'), may hold values from -6 to 6
- grad_rows: bfloat16 [2, 8, 256, 1536], P('frame', 'tile', 'section'), may hold values from -6 to 6
- offsets: int32 [12, 9, 3], P('section'), may hold values from -1 to 1, as said below
- counts: int32 [2, 8], replicated, may hold values from 8 to 256, as said below
Outputs:
- grad_query: bfloat16 [2, 8, 256, 1536], P('frame', 'tile', None, 'section')
- grad_key: bfloat16 [2, 8, 256, 1536], P('frame', 'tile', None, 'section')
- grad_value: bfloat16 [2, 8, 256, 1536], P('frame', 'tile', None, 'section')
The draws below stay inside these ranges and needn't reach their ends.
Inputs may be any that keep to these rules, and one draw needn't show every extreme that they name: `offsets`: of heads 2m and 2m + 1, one lists the nine tiles (0, a, b) and the other the nine tiles (a, b, 0), for a and b each of -1, 0, 1, each head in an order of its own. `counts`: the real tokens of a tile fill its first slots; tiles outside the last block of frames and the last row of spatial tiles are full; the last tile of the grid holds 8; a tile holds a multiple of 8 real tokens.
All inputs are finite; a program needn't handle non-finite values.
Results may differ from the reference program's by a relative error of at most 0.008.
Values may be sent and summed in bfloat16 or wider, within the bound.
No kernel may reach another device: no remote copies, remote signals or barrier semaphores. Data moves between devices by JAX's collectives and lax.ppermute only.
A program may use at most 128 MiB of HBM per device.

```python
import math
import jax
import jax.numpy as jnp
from jax import lax

H = 12
HD = 128
D = 1536
TF = 4
TH = 8
TW = 8
TILE = 256
NCT = 4
NFT = 2
NST = 8


def draw_queries(key, part):
    sample = jnp.clip(jax.random.normal(jax.random.fold_in(key, 1), (NFT, NST, TILE, H * HD)), -4.0, 4.0)
    return sample.astype(jnp.bfloat16)


def draw_key_rows(key, part):
    sample = jnp.clip(jax.random.normal(jax.random.fold_in(key, 2), (NFT, NST, TILE, H * HD)), -4.0, 4.0)
    return sample.astype(jnp.bfloat16)


def draw_offsets(key, part):
    flips = jax.random.randint(jax.random.fold_in(key, 7), (H // 2,), 0, 2)
    second_kind = jnp.stack([flips, 1 - flips], axis=1).reshape(H)
    outer_steps = jnp.repeat(jnp.arange(3, dtype=jnp.int32) - 1, 3)
    inner_steps = jnp.tile(jnp.arange(3, dtype=jnp.int32) - 1, 3)
    zeros_nine = jnp.zeros((9,), jnp.int32)
    spatial = jnp.stack([zeros_nine, outer_steps, inner_steps], axis=1)
    temporal = jnp.stack([outer_steps, inner_steps, zeros_nine], axis=1)
    table = jnp.where(second_kind[:, None, None] == 1, temporal[None], spatial[None])
    head_keys = jax.random.split(jax.random.fold_in(key, 8), H)
    orders = jax.vmap(lambda head_key: jax.random.permutation(head_key, 9))(head_keys).astype(jnp.int32)
    table = jnp.take_along_axis(table, orders[:, :, None], axis=1)
    return table.astype(jnp.int32)


def draw_counts(key, part):
    levels = jax.random.randint(jax.random.fold_in(key, 5), (NFT, NST), 1, TF * TH + 1)
    frame_ids = jnp.arange(NFT)[:, None]
    spot_ids = jnp.arange(NST)[None, :]
    row_ids = spot_ids // NCT
    border = (frame_ids == NFT - 1) | (row_ids == NST // NCT - 1)
    units = jnp.where(border, levels, TF * TH)
    units = jnp.where((frame_ids == NFT - 1) & (spot_ids == NST - 1), 1, units)
    return (units * TW).astype(jnp.int32)


def block_levels(stream_key, dims, pieces, least, top_value):
    loudness = 1.0
    for position, shards_of in pieces:
        draws = jax.random.uniform(jax.random.fold_in(jax.random.fold_in(stream_key, 6), position), (shards_of,), jnp.float32, least / len(pieces), top_value / len(pieces))
        loudness = loudness * jnp.repeat(jnp.exp(draws), dims[position] // shards_of).reshape((-1,) + (1,) * (len(dims) - 1 - position))
    return loudness


def noise(own_key, shape, scale, bound, cuts=(), held_as=jnp.bfloat16):
    loudness = block_levels(own_key, shape, cuts, -0.22, 0.18) if cuts else 1.0
    entries = jax.random.normal(own_key, shape, jnp.float32) * scale * loudness
    return jnp.minimum(jnp.maximum(entries, -bound), bound).astype(held_as)


def setup_inputs(seed: int = 0) -> dict:
    key_list = jax.random.split(jax.random.key(seed), 7)
    queries = draw_queries(jax.random.fold_in(key_list[6], 71), 0)
    key_rows = draw_key_rows(jax.random.fold_in(key_list[6], 71), 0)
    value_rows = noise(key_list[2], (NFT, NST, TILE, D), 1.0, 6.0, ((0, 2), (1, 8), (3, 2)))
    grad_rows = noise(key_list[3], (NFT, NST, TILE, D), 1.0, 6.0, ((0, 2), (1, 8), (2, 2)))
    offsets = draw_offsets(jax.random.fold_in(key_list[6], 71), 0)
    counts = draw_counts(jax.random.fold_in(key_list[6], 71), 0)
    return dict(queries=queries, key_rows=key_rows, value_rows=value_rows, grad_rows=grad_rows, offsets=offsets, counts=counts)


def reference(queries, key_rows, value_rows, grad_rows, offsets, counts):
    frame_count, spot_count, tile_len, model_width = queries.shape
    col_count = NCT
    row_count = spot_count // col_count
    head_count = offsets.shape[0]
    window = offsets.shape[1]
    head_dim = model_width // head_count
    score_scale = 1.0 / math.sqrt(head_dim)
    key_split = key_rows.reshape(frame_count, spot_count, tile_len, head_count, head_dim)
    value_split = value_rows.reshape(frame_count, spot_count, tile_len, head_count, head_dim)
    positions = jnp.arange(tile_len, dtype=jnp.int32)
    live_rows = positions[None, None, :] < counts[:, :, None]
    masked = jnp.where(live_rows[..., None], grad_rows, jnp.zeros_like(grad_rows))
    head_ids = jnp.broadcast_to(jnp.arange(head_count, dtype=jnp.int32)[:, None], (head_count, window))
    anchor = jnp.zeros((), jnp.int32)

    def one_tile(tile_at, state):
        query_out, key_total, value_total = state
        tile_at = jnp.asarray(tile_at).astype(jnp.int32)
        frame_at = (tile_at // spot_count).astype(jnp.int32)
        spot_at = (tile_at % spot_count).astype(jnp.int32)
        row_at = spot_at // col_count
        col_at = spot_at % col_count
        near_frame = frame_at + offsets[:, :, 0]
        near_row = row_at + offsets[:, :, 1]
        near_col = col_at + offsets[:, :, 2]
        inside = (near_frame >= 0) & (near_frame < frame_count) & (near_row >= 0) & (near_row < row_count) & (near_col >= 0) & (near_col < col_count)
        frame_pick = jnp.clip(near_frame, 0, frame_count - 1).astype(jnp.int32)
        spot_pick = (jnp.clip(near_row, 0, row_count - 1) * col_count + jnp.clip(near_col, 0, col_count - 1)).astype(jnp.int32)
        live_count = jnp.where(inside, counts[frame_pick, spot_pick], 0)
        live_keys = positions[None, None, :] < live_count[:, :, None]
        key_window = key_split[frame_pick, spot_pick, :, head_ids, :].astype(jnp.float32)
        value_window = value_split[frame_pick, spot_pick, :, head_ids, :].astype(jnp.float32)
        query_tile = queries[frame_at, spot_at].reshape(tile_len, head_count, head_dim).astype(jnp.float32)
        grad_tile = masked[frame_at, spot_at].reshape(tile_len, head_count, head_dim).astype(jnp.float32)
        scores = jnp.einsum('ihe,houe->hiou', query_tile, key_window) * score_scale
        scores = jnp.where(live_keys[:, None], scores, -jnp.inf)
        row_max = lax.optimization_barrier(jnp.max(scores, axis=(2, 3), keepdims=True))
        log_total = row_max + jnp.log(lax.optimization_barrier(jnp.sum(jnp.exp(scores - row_max), axis=(2, 3), keepdims=True)))
        softmax = jnp.exp(scores - log_total)
        grad_softmax = jnp.einsum('ihe,houe->hiou', grad_tile, value_window)
        row_dot = lax.optimization_barrier(jnp.sum(softmax * grad_softmax, axis=(2, 3), keepdims=True))
        grad_scores = (softmax * (grad_softmax - row_dot)).astype(jnp.bfloat16)
        softmax_low = softmax.astype(jnp.bfloat16)
        grad_scores = lax.optimization_barrier(grad_scores).astype(jnp.float32)
        softmax_low = lax.optimization_barrier(softmax_low).astype(jnp.float32)
        query_grad = jnp.einsum('hiou,houe->ihe', grad_scores, key_window) * score_scale
        query_grad = query_grad.reshape(1, 1, tile_len, model_width).astype(jnp.bfloat16)
        query_out = lax.dynamic_update_slice(query_out, query_grad, (frame_at, spot_at, anchor, anchor))
        value_part = jnp.einsum('hiou,ihe->houe', softmax_low, grad_tile)
        key_part = jnp.einsum('hiou,ihe->houe', grad_scores, query_tile) * score_scale
        key_total = key_total.at[frame_pick, spot_pick, :, head_ids, :].add(key_part)
        value_total = value_total.at[frame_pick, spot_pick, :, head_ids, :].add(value_part)
        return (query_out, key_total, value_total)
    start = (jnp.zeros_like(queries), jnp.zeros((frame_count, spot_count, tile_len, head_count, head_dim), jnp.float32), jnp.zeros((frame_count, spot_count, tile_len, head_count, head_dim), jnp.float32))
    query_out, key_total, value_total = lax.fori_loop(0, frame_count * spot_count, one_tile, start)
    grad_key = key_total.reshape(frame_count, spot_count, tile_len, model_width).astype(jnp.bfloat16)
    grad_value = value_total.reshape(frame_count, spot_count, tile_len, model_width).astype(jnp.bfloat16)
    return (query_out, grad_key, grad_value)
```

```python
import functools
import math

import jax
import jax.numpy as jnp
from jax import lax
from jax.experimental import pallas as pl
from jax.experimental.pallas import tpu as pltpu
from jax.sharding import PartitionSpec as P

NCT = 4
LOG2E = 1.4426950408889634
DEAD = -1e30
VMEM_LIMIT = 48 * 1024 * 1024

SMEM = pl.BlockSpec(memory_space=pltpu.SMEM)
NT = (((1,), (1,)), ((), ()))
NN = (((1,), (0,)), ((), ()))
TN = (((0,), (0,)), ((), ()))


def dot(a, b, dims):
    return lax.dot_general(a, b, dims, preferred_element_type=jnp.float32)


def steps_along(size):
    if size == 1:
        return []
    if size == 2:
        return [[1, 0]]
    return [
        [p - 1 if p > 0 else None for p in range(size)],
        [p + 1 if p + 1 < size else None for p in range(size)],
    ]


def row_route(step, col_count):
    return [
        (source * col_count + col, row * col_count + col)
        for row, source in enumerate(step)
        if source is not None
        for col in range(col_count)
    ]


def col_route(step, row_count):
    col_count = len(step)
    return [
        (row * col_count + source, row * col_count + col)
        for col, source in enumerate(step)
        if source is not None
        for row in range(row_count)
    ]


def frame_route(step):
    return [(source, frame) for frame, source in enumerate(step) if source is not None]


def reverse(route):
    return [(b, a) for a, b in route]


def source_of(step, place):
    if len(step) == 2:
        return 1 - place, True
    if step[0] is None:
        return jnp.maximum(place - 1, 0), place > 0
    return jnp.minimum(place + 1, len(step) - 1), place + 1 < len(step)


def slot_counts(counts_ref, frame_steps, col_steps, col_count):
    frame = lax.axis_index("frame")
    spot = lax.axis_index("tile")
    row = lax.div(spot, col_count)
    col = lax.rem(spot, col_count)
    own = counts_ref[frame, spot]
    plane, across = [own], [own]
    for step in col_steps:
        source, there = source_of(step, col)
        plane.append(jnp.where(there, counts_ref[frame, row * col_count + source], 0))
    for step in frame_steps:
        source, there = source_of(step, frame)
        across.append(jnp.where(there, counts_ref[source, spot], 0))
    return plane, across


def pair_flip(offsets_ref, pair):
    hits = jnp.int32(0)
    for slot in range(offsets_ref.shape[1]):
        hits = hits | jnp.abs(offsets_ref[2 * pair, slot, 0])
    return jnp.where(hits != 0, 1, 0).astype(jnp.int32)


def pack_kernel(pairs, hd, offsets_ref, k_ref, v_ref, plane_ref, across_ref):
    for pair in range(pairs):
        flip = pair_flip(offsets_ref, pair)
        first = pl.ds(pl.multiple_of(2 * pair * hd + flip * hd, hd), hd)
        second = pl.ds(pl.multiple_of(2 * pair * hd + (1 - flip) * hd, hd), hd)
        at = pl.ds(pair * hd, hd)
        for i, ref in enumerate((k_ref, v_ref)):
            plane_ref[i, :, at] = ref[:, first]
            across_ref[i, :, at] = ref[:, second]


def gather_kernel(sections, pairs, counts_ref, grad_ref, *refs):
    got_refs, out_refs = refs[: sections - 1], refs[sections - 1 :]
    section = lax.axis_index("section")
    count = counts_ref[lax.axis_index("frame"), lax.axis_index("tile")]
    rows, width = got_refs[0].shape if got_refs else grad_ref.shape
    pair_width = width // pairs
    at_rows = lax.broadcasted_iota(jnp.int32, (rows, 1), 0)
    for k in range(sections):
        holder = lax.rem(section + sections - k, sections)
        live = at_rows + holder * rows < count
        start = pl.multiple_of(holder * rows, rows)
        for pair in range(pairs):
            if k == 0:
                at = pl.multiple_of(section * width + pair * pair_width, pair_width)
                part = grad_ref[:, pl.ds(at, pair_width)]
            else:
                part = got_refs[k - 1][:, pl.ds(pair * pair_width, pair_width)]
            part = jnp.where(live, part.astype(jnp.float32), 0.0).astype(part.dtype)
            out_refs[pair][pl.ds(start, rows), :] = part


class Window:
    def __init__(self, plan, refs):
        refs = list(refs)
        self.plan = plan
        take = lambda n: [refs.pop(0) for _ in range(n)]
        self.offsets, self.counts = take(2)
        self.q = take(1 + plan.nr)
        self.grad = take(1 + plan.nr)
        self.k, self.v = take(2)
        self.near_plane = take(plan.nc)
        self.near_across = take(plan.nf)
        self.rest = refs

    def heads(self):
        plan = self.plan
        hd = plan.hd
        flip = pair_flip(self.offsets, plan.pair)
        plane_counts, across_counts = slot_counts(
            self.counts, plan.frame_steps, plan.col_steps, plan.col_count
        )
        for kind, near, live in (
            (0, self.near_plane, plane_counts),
            (1, self.near_across, across_counts),
        ):
            at = flip if kind == 0 else 1 - flip
            cols = pl.ds(pl.multiple_of(at * hd, hd), hd)
            q = jnp.concatenate([ref[:, cols] for ref in self.q], axis=0)
            grad = jnp.concatenate([ref[:, cols] for ref in self.grad], axis=0)
            slots = [(self.k[:, cols], self.v[:, cols])]
            slots += [(ref[0], ref[1]) for ref in near]
            yield kind, cols, q, grad, list(zip(slots, live))


def masked_scores(key, q, count, factor):
    scores = dot(key, q, NT) * factor
    live = lax.broadcasted_iota(jnp.int32, (key.shape[0], 1), 0) < count
    return jnp.where(live, scores, DEAD)


def merge(parts):
    top = functools.reduce(jnp.maximum, [m for m, _, _ in parts])
    weights = [jnp.exp2(m - top) for m, _, _ in parts]
    total = sum(w * l for w, (_, l, _) in zip(weights, parts))
    cross = sum(w * t for w, (_, _, t) in zip(weights, parts))
    return top, total, cross


def stats_kernel(plan, *refs):
    window = Window(plan, refs)
    (out_ref,) = window.rest
    rows = []
    for kind, cols, q, grad, slots in window.heads():
        parts = []
        for (key, value), count in slots:
            scores = masked_scores(key, q, count, plan.factor)
            top = jnp.max(scores, axis=0, keepdims=True)
            weight = jnp.exp2(scores - top)
            total = jnp.sum(weight, axis=0, keepdims=True)
            cross = jnp.sum(weight * dot(value, grad, NT), axis=0, keepdims=True)
            parts.append((top, total, cross))
        rows += list(merge(parts))
        rows.append(jnp.zeros_like(rows[0]))
    out_ref[...] = jnp.concatenate(rows, axis=0)


def grads_kernel(plan, *refs):
    window = Window(plan, refs)
    rest = list(window.rest)
    stats = [rest.pop(0)[...] for _ in range(plan.n_stats)]
    if plan.n_stats == 2:
        half = plan.tile
        stats[1] = jnp.concatenate([stats[1][:, half:], stats[1][:, :half]], axis=1)
    dq_refs = [rest.pop(0) for _ in range(1 + plan.nr)]
    dk_ref, dv_ref = rest.pop(0), rest.pop(0)
    near_refs = ([rest.pop(0) for _ in range(plan.nc)], [rest.pop(0) for _ in range(plan.nf)])
    tile, hd = plan.tile, plan.hd
    for kind, cols, q, grad, slots in window.heads():
        base = 4 * kind
        parts = [tuple(s[base + i : base + i + 1, :] for i in range(3)) for s in stats]
        top, total, cross = merge(parts)
        log_total = top + jnp.log(total) * LOG2E
        row_dot = cross / total
        query_grad = None
        for at, ((key, value), count) in enumerate(slots):
            scores = masked_scores(key, q, count, plan.factor)
            softmax = jnp.exp2(scores - log_total)
            grad_softmax = dot(value, grad, NT)
            grad_scores = (softmax * (grad_softmax - row_dot)).astype(jnp.bfloat16)
            dv = dot(softmax.astype(jnp.bfloat16), grad, NN)
            dk = dot(grad_scores, q, NN) * plan.scale
            term = dot(key, grad_scores, TN)
            query_grad = term if query_grad is None else query_grad + term
            if at == 0:
                dk_ref[:, cols] = dk
                dv_ref[:, cols] = dv
            else:
                near_refs[kind][at - 1][0] = dk.astype(jnp.bfloat16)
                near_refs[kind][at - 1][1] = dv.astype(jnp.bfloat16)
        query_grad = jnp.transpose(query_grad * plan.scale)
        for at, ref in enumerate(dq_refs):
            ref[:, cols] = query_grad[at * tile : (at + 1) * tile].astype(ref.dtype)


def finish_kernel(plan, pairs, offsets_ref, *refs):
    refs = list(refs)
    take = lambda n: [refs.pop(0) for _ in range(n)]
    tile, hd = plan.tile, plan.hd
    per_pair = [(take(1 + plan.nr), take(2), take(plan.nc), take(plan.nf)) for _ in range(pairs)]
    dq_ref, dk_ref, dv_ref = refs
    for pair, (dq, own, near_plane, near_across) in enumerate(per_pair):
        at = pl.ds(pair * 2 * hd, 2 * hd)
        total = dq[0][...]
        for ref in dq[1:]:
            total = total + ref[...].astype(jnp.float32)
        dq_ref[:, at] = total.astype(dq_ref.dtype)
        flip = pair_flip(offsets_ref, pair)
        for kind, near in ((0, near_plane), (1, near_across)):
            place = flip if kind == 0 else 1 - flip
            cols = pl.ds(pl.multiple_of(place * hd, hd), hd)
            out_cols = pl.ds(pl.multiple_of((2 * pair + place) * hd, hd), hd)
            for i, out in enumerate((dk_ref, dv_ref)):
                total = own[i][:, cols]
                for ref in near:
                    total = total + ref[i].astype(jnp.float32)
                out[:, out_cols] = total.astype(out.dtype)


class Plan:
    pass


def params():
    return pltpu.CompilerParams(vmem_limit_bytes=VMEM_LIMIT)


def local(queries, key_rows, value_rows, grad_rows, offsets, counts):
    q, k, v, grad = queries[0, 0], key_rows[0, 0], value_rows[0, 0], grad_rows[0, 0]
    tile, width = q.shape
    heads = offsets.shape[0]
    pairs = heads // 2
    hd = width // heads
    sections = lax.axis_size("section")
    frame_count = lax.axis_size("frame")
    col_count = NCT
    row_count = lax.axis_size("tile") // col_count

    plan = Plan()
    plan.tile, plan.hd, plan.col_count = tile, hd, col_count
    plan.scale = 1.0 / math.sqrt(hd)
    plan.factor = plan.scale * LOG2E
    row_steps = steps_along(row_count)
    plan.col_steps = steps_along(col_count)
    plan.frame_steps = steps_along(frame_count)
    plan.nr, plan.nc, plan.nf = len(row_steps), len(plan.col_steps), len(plan.frame_steps)
    row_routes = [row_route(step, col_count) for step in row_steps]
    col_routes = [col_route(step, row_count) for step in plan.col_steps]
    frame_routes = [frame_route(step) for step in plan.frame_steps]

    def from_rows(x):
        return [lax.ppermute(x, "tile", route) for route in row_routes]

    far_q = from_rows(q)

    section = lax.axis_index("section")
    got = []
    for shift in range(1, sections):
        target = lax.rem(section + shift, sections)
        part = lax.dynamic_slice_in_dim(grad, target * width, width, 1)
        route = [(i, (i + shift) % sections) for i in range(sections)]
        got.append(lax.ppermute(part, "section", route))
    pair_shape = jax.ShapeDtypeStruct((tile, 2 * hd), jnp.bfloat16)
    vm = pl.BlockSpec(memory_space=pltpu.VMEM)
    grads = pl.pallas_call(
        functools.partial(gather_kernel, sections, pairs),
        out_shape=[pair_shape] * pairs,
        in_specs=[SMEM] + [vm] * sections,
        out_specs=[vm] * pairs,
        compiler_params=params(),
        name="gather_grad",
    )(counts, grad, *got)

    packed = jax.ShapeDtypeStruct((2, tile, pairs * hd), jnp.bfloat16)
    plane_kv, across_kv = pl.pallas_call(
        functools.partial(pack_kernel, pairs, hd),
        out_shape=[packed, packed],
        in_specs=[SMEM, vm, vm],
        out_specs=[vm, vm],
        compiler_params=params(),
        name="pack_kv",
    )(offsets, k, v)
    near_plane = [lax.ppermute(plane_kv, "tile", route) for route in col_routes]
    near_across = [lax.ppermute(across_kv, "frame", route) for route in frame_routes]
    far_grads = [from_rows(g) for g in grads]

    nq = 1 + plan.nr
    blocks = 2 * nq + plan.nc + plan.nf
    half_cost = 2 * 2 * nq * (2 + plan.nc + plan.nf) * tile * tile * hd
    done = []
    for pair in range(pairs):
        plan_m = Plan()
        plan_m.__dict__.update(plan.__dict__)
        plan_m.pair = pair
        wide = pl.BlockSpec((tile, 2 * hd), lambda i, pair=pair: (0, pair))
        whole = pl.BlockSpec((tile, 2 * hd), lambda i: (0, 0))
        kv = pl.BlockSpec((2, tile, hd), lambda i, pair=pair: (0, 0, pair))
        kv_out = pl.BlockSpec((2, tile, hd), lambda i: (0, 0, 0))
        stat = pl.BlockSpec((8, nq * tile), lambda i: (0, 0))
        operands = [offsets, counts, q, *far_q, grads[pair], *far_grads[pair], k, v]
        operands += near_plane + near_across
        specs = [SMEM, SMEM] + [wide] * nq + [whole] * nq + [wide] * 2 + [kv] * (plan.nc + plan.nf)
        stats = pl.pallas_call(
            functools.partial(stats_kernel, plan_m),
            grid=(1,),
            out_shape=jax.ShapeDtypeStruct((8, nq * tile), jnp.float32),
            in_specs=specs,
            out_specs=stat,
            compiler_params=params(),
            cost_estimate=pl.CostEstimate(flops=half_cost, bytes_accessed=2 << 20, transcendentals=0),
            name="row_totals",
        )(*operands)
        all_stats = share_stats(stats, row_routes, tile)
        plan_m.n_stats = len(all_stats)
        f32_pair = jax.ShapeDtypeStruct((tile, 2 * hd), jnp.float32)
        near_out = jax.ShapeDtypeStruct((2, tile, hd), jnp.bfloat16)
        outs = pl.pallas_call(
            functools.partial(grads_kernel, plan_m),
            grid=(1,),
            out_shape=[f32_pair] + [pair_shape] * plan.nr + [f32_pair] * 2 + [near_out] * (plan.nc + plan.nf),
            in_specs=specs + [stat] * len(all_stats),
            out_specs=[whole] * (nq + 2) + [kv_out] * (plan.nc + plan.nf),
            compiler_params=params(),
            cost_estimate=pl.CostEstimate(flops=half_cost * 5 // 2, bytes_accessed=4 << 20, transcendentals=0),
            name="pair_grads",
        )(*operands, *all_stats)
        own_q, far_out = outs[0], outs[1:nq]
        own_kv = outs[nq : nq + 2]
        plane_out = outs[nq + 2 : nq + 2 + plan.nc]
        across_out = outs[nq + 2 + plan.nc :]
        back_q = [lax.ppermute(x, "tile", reverse(r)) for x, r in zip(far_out, row_routes)]
        back_plane = [lax.ppermute(x, "tile", reverse(r)) for x, r in zip(plane_out, col_routes)]
        back_across = [lax.ppermute(x, "frame", reverse(r)) for x, r in zip(across_out, frame_routes)]
        done += [own_q, *back_q, *own_kv, *back_plane, *back_across]

    out = jax.ShapeDtypeStruct((tile, width), jnp.bfloat16)
    dq, dk, dv = pl.pallas_call(
        functools.partial(finish_kernel, plan, pairs),
        out_shape=[out] * 3,
        in_specs=[SMEM] + [vm] * len(done),
        out_specs=[vm] * 3,
        compiler_params=params(),
        name="add_terms",
    )(offsets, *done)
    return dq[None, None], dk[None, None], dv[None, None]


def share_stats(stats, row_routes, tile):
    if len(row_routes) == 0:
        return [stats]
    if len(row_routes) == 1:
        return [stats, lax.ppermute(stats, "tile", row_routes[0])]
    terms = [stats[:, :tile]]
    for at, route in enumerate(row_routes):
        part = stats[:, (at + 1) * tile : (at + 2) * tile]
        terms.append(lax.ppermute(part, "tile", reverse(route)))
    merged = []
    for base in (0, 4):
        parts = [(t[base], t[base + 1], t[base + 2]) for t in terms]
        parts = [(jnp.where(l > 0, m, DEAD), l, t) for m, l, t in parts]
        merged += list(merge(parts))
        merged.append(jnp.ones_like(merged[0]))
    totals = jnp.stack(merged)
    shared = [totals] + [lax.ppermute(totals, "tile", route) for route in row_routes]
    return [jnp.concatenate(shared, axis=1)]


def solution(mesh):
    return jax.shard_map(
        local,
        mesh=mesh,
        in_specs=(
            P("frame", "tile", None, "section"),
            P("frame", "tile", None, "section"),
            P("frame", "tile", None, "section"),
            P("frame", "tile", "section", None),
            P("section", None, None),
            P(),
        ),
        out_specs=(
            P("frame", "tile", None, "section"),
            P("frame", "tile", None, "section"),
            P("frame", "tile", None, "section"),
        ),
        check_vma=False,
    )
```

```python
import functools
import math

import jax
import jax.numpy as jnp
from jax import lax
from jax.experimental import pallas as pl
from jax.experimental.pallas import tpu as pltpu
from jax.sharding import PartitionSpec as P

NCT = 4
LOG2E = 1.4426950408889634
DEAD = -1e30
VMEM_LIMIT = 24 * 1024 * 1024

SMEM = pl.BlockSpec(memory_space=pltpu.SMEM)
NT = (((1,), (1,)), ((), ()))
NN = (((1,), (0,)), ((), ()))
TN = (((0,), (0,)), ((), ()))


def dot(a, b, dims):
    return lax.dot_general(a, b, dims, preferred_element_type=jnp.float32)


def swaps_along(size):
    return [
        [(p, p + 1) for p in range(first, size - 1, 2)] for first in (0, 1) if first + 1 < size
    ]


def both_ways(pairs):
    return [(a, b) for a, b in pairs] + [(b, a) for a, b in pairs]


def row_route(swap, col_count):
    return [
        (a * col_count + col, b * col_count + col)
        for a, b in both_ways(swap)
        for col in range(col_count)
    ]


def col_route(swap, row_count, col_count):
    return [
        (row * col_count + a, row * col_count + b)
        for a, b in both_ways(swap)
        for row in range(row_count)
    ]


def partner(at, place, size):
    other = jnp.where(lax.rem(place, 2) == at, place + 1, place - 1)
    return jnp.clip(other, 0, size - 1), (other >= 0) & (other < size)


def table_rows(plan):
    cols = 1
    frames = cols + plan.nc
    rows = frames + plan.nf
    flips = rows + plan.nr
    return cols, frames, rows, flips


def table_shape(plan):
    rows = table_rows(plan)[-1] + plan.pairs
    return jax.ShapeDtypeStruct((-(-rows // 8) * 8, plan.hd), jnp.int32)


def prepare_kernel(plan, offsets_ref, counts_ref, q_ref, k_ref, v_ref, *refs):
    table_ref, plane_ref, across_ref, q_out_ref = refs
    hd = plan.hd
    frame, spot = lax.axis_index("frame"), lax.axis_index("tile")
    row, col = lax.div(spot, plan.col_count), lax.rem(spot, plan.col_count)
    entries = [counts_ref[frame, spot]]
    for at in range(plan.nc):
        other, there = partner(at, col, plan.col_count)
        entries.append(jnp.where(there, counts_ref[frame, row * plan.col_count + other], 0))
    for at in range(plan.nf):
        other, there = partner(at, frame, plan.frame_count)
        entries.append(jnp.where(there, counts_ref[other, spot], 0))
    for at in range(plan.nr):
        other, there = partner(at, row, plan.row_count)
        entries.append(jnp.where(there, counts_ref[frame, other * plan.col_count + col], 0))
    for pair in range(plan.pairs):
        hits = jnp.int32(0)
        for slot in range(offsets_ref.shape[1]):
            hits = hits | jnp.abs(offsets_ref[2 * pair, slot, 0])
        flip = jnp.where(hits != 0, 1, 0).astype(jnp.int32)
        entries.append(flip)
        first = pl.ds(pl.multiple_of(2 * pair * hd + flip * hd, hd), hd)
        second = pl.ds(pl.multiple_of(2 * pair * hd + (1 - flip) * hd, hd), hd)
        at = pl.ds(pair * hd, hd)
        for i, ref in enumerate((k_ref, v_ref)):
            plane_ref[i, :, at] = ref[:, first]
            across_ref[i, :, at] = ref[:, second]
        q_out_ref[:, pl.ds(2 * pair * hd, hd)] = q_ref[:, first]
        q_out_ref[:, pl.ds((2 * pair + 1) * hd, hd)] = q_ref[:, second]
    entries += [jnp.int32(0)] * (table_ref.shape[0] - len(entries))
    for at, entry in enumerate(entries):
        table_ref[at : at + 1, :] = jnp.full((1, hd), entry, jnp.int32)


def gather_kernel(plan, swap, table_ref, grad_ref, *refs):
    refs = list(refs)
    if swap is not None:
        q_ref, q_out_ref = refs.pop(0), refs.pop()
    got_refs, out_ref = refs[:-1], refs[-1]
    section = lax.axis_index("section")
    sections = len(refs)
    _, _, row_rows, flip_rows = table_rows(plan)
    at = 0 if swap is None else row_rows + swap
    count = table_ref[at : at + 1, :]
    rows, width, hd = grad_ref.shape[0], out_ref.shape[1], plan.hd
    at_rows = lax.broadcasted_iota(jnp.int32, (rows, hd), 0)
    for k in range(sections):
        holder = lax.rem(section + sections - k, sections)
        live = at_rows + holder * rows < count
        start = pl.multiple_of(holder * rows, rows)
        for pair in range(plan.pairs):
            heads = []
            for head in (2 * pair, 2 * pair + 1):
                if k == 0:
                    at = pl.multiple_of(section * width + head * hd, hd)
                    part = grad_ref[:, pl.ds(at, hd)]
                else:
                    part = got_refs[k - 1][:, pl.ds(head * hd, hd)]
                heads.append(jnp.where(live, part.astype(jnp.float32), 0.0))
            for i, part in enumerate(in_order(table_ref, flip_rows + pair, *heads)):
                part = part.astype(out_ref.dtype)
                out_ref[pl.ds(start, rows), pl.ds((2 * pair + i) * hd, hd)] = part


    if swap is not None:
        for pair in range(plan.pairs):
            cols = [pl.ds((2 * pair + i) * hd, hd) for i in (0, 1)]
            heads = [q_ref[:, at].astype(jnp.float32) for at in cols]
            for at, part in zip(cols, in_order(table_ref, flip_rows + pair, *heads)):
                q_out_ref[:, at] = part.astype(q_out_ref.dtype)


def in_order(table_ref, row, a, b):
    flip = jnp.broadcast_to(table_ref[row : row + 1, :], a.shape) != 0
    return jnp.where(flip, b, a), jnp.where(flip, a, b)


class Window:
    def __init__(self, plan, refs, own=True, far=True):
        refs = list(refs)
        self.plan = plan
        take = lambda n: [refs.pop(0) for _ in range(n)]
        (self.table,) = take(1)
        self.q = take((1 if own else 0) + (plan.nr if far else 0))
        self.grad = take((1 if own else 0) + (plan.nr if far else 0))
        self.kv = [take(1 + plan.nc), take(1 + plan.nf)]
        self.rest = refs

    def heads(self, pair):
        plan = self.plan
        hd, tile = plan.hd, plan.tile
        cols, frames, _, _ = table_rows(plan)
        at_rows = lax.broadcasted_iota(jnp.int32, (tile, hd), 0)
        near_at = pl.ds(pair * hd, hd)
        for kind, first in ((0, cols), (1, frames)):
            q = [ref[:, pl.ds((2 * pair + kind) * hd, hd)] for ref in self.q]
            grad = [ref[:, pl.ds((2 * pair + kind) * hd, hd)] for ref in self.grad]
            slots = []
            for at, ref in enumerate(self.kv[kind]):
                row = 0 if at == 0 else first + at - 1
                bias = jnp.where(at_rows < self.table[row : row + 1, :], 0.0, DEAD)
                bias = jnp.concatenate([bias] * (len(q) * tile // hd), axis=1)
                slots.append((ref[0, :, near_at], ref[1, :, near_at], bias))
            yield kind, jnp.concatenate(q, axis=0), jnp.concatenate(grad, axis=0), slots


def merge(parts):
    top = functools.reduce(jnp.maximum, [m for m, _, _ in parts])
    weights = [jnp.exp2(m - top) for m, _, _ in parts]
    total = sum(w * l for w, (_, l, _) in zip(weights, parts))
    cross = sum(w * t for w, (_, _, t) in zip(weights, parts))
    return top, total, cross


def row_stats(window, pair):
    rows = []
    for kind, q, grad, slots in window.heads(pair):
        parts = []
        for key, value, bias in slots:
            scores = dot(key, q, NT) * window.plan.factor + bias
            top = jnp.max(scores, axis=0, keepdims=True)
            weight = jnp.exp2(scores - top)
            total = jnp.sum(weight, axis=0, keepdims=True)
            cross = jnp.sum(weight * dot(value, grad, NT), axis=0, keepdims=True)
            parts.append((top, total, cross))
        rows += list(merge(parts))
        rows.append(jnp.zeros_like(rows[0]))
    return jnp.concatenate(rows, axis=0)


def own_stats_kernel(plan, *refs):
    pairs = range(plan.pairs)
    window = Window(plan, refs, far=False)
    (out_ref,) = window.rest
    for pair in pairs:
        out_ref[pair] = row_stats(window, pair)


def far_stats_kernel(plan, *refs):
    window = Window(plan, refs, own=False)
    own_ref, out_ref = window.rest
    for at, pair in enumerate(plan.group):
        out_ref[at, :, : plan.tile] = own_ref[pair]
        out_ref[at, :, plan.tile :] = row_stats(window, pair)


def grads_kernel(plan, *refs):
    window = Window(plan, refs)
    rest = list(window.rest)
    take = lambda n: [rest.pop(0) for _ in range(n)]
    stats_refs = take(plan.n_stats)
    dq_refs = take(1 + plan.nr)
    own_refs = take(2)
    near_refs = [take(plan.nc), take(plan.nf)]
    tile, hd = plan.tile, plan.hd
    for behind, pair in enumerate(plan.part):
        stats = [ref[plan.group.index(pair)] for ref in stats_refs]
        if plan.n_stats == 2:
            stats[1] = jnp.concatenate([stats[1][:, tile:], stats[1][:, :tile]], axis=1)
        near_at = pl.ds(behind * hd, hd)
        for kind, q, grad, slots in window.heads(pair):
            base = 4 * kind
            cols = pl.ds((2 * behind + kind) * hd, hd)
            parts = [tuple(s[base + i : base + i + 1, :] for i in range(3)) for s in stats]
            top, total, cross = merge(parts)
            log_total = top + jnp.log(total) * LOG2E
            row_dot = cross / total
            query_grad = None
            for at, (key, value, bias) in enumerate(slots):
                scores = dot(key, q, NT) * plan.factor + bias
                softmax = jnp.exp2(scores - log_total)
                grad_softmax = dot(value, grad, NT)
                grad_scores = (softmax * (grad_softmax - row_dot)).astype(jnp.bfloat16)
                dk = dot(grad_scores, q, NN) * plan.scale
                dv = dot(softmax.astype(jnp.bfloat16), grad, NN)
                term = dot(key, grad_scores, TN)
                query_grad = term if query_grad is None else query_grad + term
                for i, out in enumerate((dk, dv)):
                    if at == 0:
                        own_refs[i][:, cols] = out
                    else:
                        near_refs[kind][at - 1][i, :, near_at] = out.astype(jnp.bfloat16)
            query_grad = jnp.transpose(query_grad * plan.scale)
            for at, ref in enumerate(dq_refs):
                ref[:, cols] = query_grad[at * tile : (at + 1) * tile].astype(ref.dtype)


def finish_kernel(plan, parts, table_ref, *refs):
    refs = list(refs)
    take = lambda n: [refs.pop(0) for _ in range(n)]
    hd = plan.hd
    flip_rows = table_rows(plan)[-1]
    per_part = [(part, take(1 + plan.nr), take(2), take(plan.nc), take(plan.nf)) for part in parts]
    dq_ref, dk_ref, dv_ref = refs

    def put(out_ref, pair, kinds):
        for i, part in enumerate(in_order(table_ref, flip_rows + pair, *kinds)):
            out_ref[:, pl.ds((2 * pair + i) * hd, hd)] = part.astype(out_ref.dtype)

    for part, dq, own, *near in per_part:
        for behind, pair in enumerate(part):
            near_at = pl.ds(behind * hd, hd)
            cols = [pl.ds((2 * behind + kind) * hd, hd) for kind in (0, 1)]
            put(dq_ref, pair, [sum(ref[:, at].astype(jnp.float32) for ref in dq) for at in cols])
            for i, out in enumerate((dk_ref, dv_ref)):
                kinds = []
                for kind in (0, 1):
                    total = own[i][:, cols[kind]]
                    for ref in near[kind]:
                        total = total + ref[i, :, near_at].astype(jnp.float32)
                    kinds.append(total)
                put(out, pair, kinds)


class Plan:
    pass


def split_pairs(pairs):
    return [list(range(pairs))]


def params():
    return pltpu.CompilerParams(vmem_limit_bytes=VMEM_LIMIT)


def local(queries, key_rows, value_rows, grad_rows, offsets, counts):
    q, k, v, grad = queries[0, 0], key_rows[0, 0], value_rows[0, 0], grad_rows[0, 0]
    tile, width = q.shape
    heads = offsets.shape[0]
    pairs = heads // 2
    hd = width // heads
    sections = lax.axis_size("section")
    frame_count = lax.axis_size("frame")
    col_count = NCT
    row_count = lax.axis_size("tile") // col_count

    plan = Plan()
    plan.tile, plan.hd, plan.col_count = tile, hd, col_count
    plan.scale = 1.0 / math.sqrt(hd)
    plan.factor = plan.scale * LOG2E
    row_swaps = swaps_along(row_count)
    col_swaps = swaps_along(col_count)
    frame_swaps = swaps_along(frame_count)
    plan.nr, plan.nc, plan.nf = len(row_swaps), len(col_swaps), len(frame_swaps)
    plan.frame_count = frame_count
    row_routes = [row_route(swap, col_count) for swap in row_swaps]
    col_routes = [col_route(swap, row_count, col_count) for swap in col_swaps]
    frame_routes = [both_ways(swap) for swap in frame_swaps]

    def from_rows(x):
        return [lax.ppermute(x, "tile", route) for route in row_routes]

    vm = pl.BlockSpec(memory_space=pltpu.VMEM)
    plan.row_count = row_count

    plan.pairs = pairs

    def call(kernel, name, out_shape, flops, *operands, scalars=()):
        many = isinstance(out_shape, list)
        return pl.pallas_call(
            kernel,
            out_shape=out_shape,
            in_specs=[SMEM] * len(scalars) + [vm] * len(operands),
            out_specs=[vm] * len(out_shape) if many else vm,
            compiler_params=params(),
            cost_estimate=pl.CostEstimate(
                flops=flops, bytes_accessed=1 << 20, transcendentals=0
            ),
            name=name,
        )(*scalars, *operands)

    low = jax.ShapeDtypeStruct((tile, width), jnp.bfloat16)

    far_raw = from_rows(grad)
    far_q_raw = from_rows(q)
    packed = jax.ShapeDtypeStruct((2, tile, pairs * hd), jnp.bfloat16)
    table, plane_kv, across_kv, own_q = call(
        functools.partial(prepare_kernel, plan),
        "prepare",
        [table_shape(plan), packed, packed, low],
        0,
        *(q, k, v),
        scalars=(offsets, counts),
    )
    section = lax.axis_index("section")

    def all_slots(raw, swap, *queries):
        got = []
        for shift in range(1, sections):
            target = lax.rem(section + shift, sections)
            part = lax.dynamic_slice_in_dim(raw, target * width, width, 1)
            route = [(i, (i + shift) % sections) for i in range(sections)]
            got.append(lax.ppermute(part, "section", route))
        return call(
            functools.partial(gather_kernel, plan, swap),
            "gather_grad",
            [low] * (1 + len(queries)),
            0,
            *(table, raw, *queries, *got),
        )

    (own_grad,) = all_slots(grad, None)
    near_plane = [lax.ppermute(plane_kv, "tile", route) for route in col_routes]
    near_across = [lax.ppermute(across_kv, "frame", route) for route in frame_routes]
    kv = [plane_kv, *near_plane, across_kv, *near_across]
    n_near = plan.nc + plan.nf
    far = [all_slots(raw, swap, far_q_raw[swap]) for swap, raw in enumerate(far_raw)]
    far_grad, far_q = [pair[0] for pair in far], [pair[1] for pair in far]

    nq = 1 + plan.nr
    quarter = 2 * 2 * (2 + n_near) * tile * tile * hd

    own_stats = call(
        functools.partial(own_stats_kernel, plan),
        "own_totals",
        jax.ShapeDtypeStruct((pairs, 8, tile), jnp.float32),
        quarter * pairs,
        *(table, own_q, own_grad, *kv),
    )
    parts = split_pairs(pairs)
    plan.group = list(range(pairs))
    stats = call(
        functools.partial(far_stats_kernel, plan),
        "far_totals",
        jax.ShapeDtypeStruct((pairs, 8, nq * tile), jnp.float32),
        quarter * plan.nr * pairs,
        *(table, *far_q, *far_grad, *kv, own_stats),
    )
    all_stats = share_stats(stats, row_routes, tile)
    plan.n_stats = len(all_stats)
    done = []
    for part in parts:
        plan_m = Plan()
        plan_m.__dict__.update(plan.__dict__)
        plan_m.part = part
        part_low = jax.ShapeDtypeStruct((tile, len(part) * 2 * hd), jnp.bfloat16)
        part_f32 = jax.ShapeDtypeStruct((tile, len(part) * 2 * hd), jnp.float32)
        near_out = jax.ShapeDtypeStruct((2, tile, len(part) * hd), jnp.bfloat16)
        outs = call(
            functools.partial(grads_kernel, plan_m),
            "pair_grads",
            [part_f32] + [part_low] * plan.nr + [part_f32] * 2 + [near_out] * n_near,
            quarter * nq * 5 // 2 * len(part),
            *(table, own_q, *far_q, own_grad, *far_grad, *kv, *all_stats),
        )
        plane_out, across_out = outs[nq + 2 : nq + 2 + plan.nc], outs[nq + 2 + plan.nc :]
        done += [outs[0]]
        done += [lax.ppermute(x, "tile", r) for x, r in zip(outs[1:nq], row_routes)]
        done += outs[nq : nq + 2]
        done += [lax.ppermute(x, "tile", r) for x, r in zip(plane_out, col_routes)]
        done += [lax.ppermute(x, "frame", r) for x, r in zip(across_out, frame_routes)]

    dq, dk, dv = call(
        functools.partial(finish_kernel, plan, parts), "add_terms", [low] * 3, 0, table, *done
    )
    return dq[None, None], dk[None, None], dv[None, None]


def share_stats(stats, row_routes, tile):
    if len(row_routes) == 0:
        return [stats]
    if len(row_routes) == 1:
        return [stats, lax.ppermute(stats, "tile", row_routes[0])]
    terms = [stats[:, :, :tile]]
    for at, route in enumerate(row_routes):
        part = stats[:, :, (at + 1) * tile : (at + 2) * tile]
        terms.append(lax.ppermute(part, "tile", route))
    merged = []
    for base in (0, 4):
        parts = [(t[:, base], t[:, base + 1], t[:, base + 2]) for t in terms]
        parts = [(jnp.where(l > 0, m, DEAD), l, t) for m, l, t in parts]
        merged += list(merge(parts))
        merged.append(jnp.ones_like(merged[0]))
    totals = jnp.stack(merged, axis=1)
    shared = [totals] + [lax.ppermute(totals, "tile", route) for route in row_routes]
    return [jnp.concatenate(shared, axis=2)]


def solution(mesh):
    return jax.shard_map(
        local,
        mesh=mesh,
        in_specs=(
            P("frame", "tile", None, "section"),
            P("frame", "tile", None, "section"),
            P("frame", "tile", None, "section"),
            P("frame", "tile", "section", None),
            P("section", None, None),
            P(),
        ),
        out_specs=(
            P("frame", "tile", None, "section"),
            P("frame", "tile", None, "section"),
            P("frame", "tile", None, "section"),
        ),
        check_vma=False,
    )
```

```python
import functools
import math

import jax
import jax.numpy as jnp
from jax import lax
from jax.experimental import pallas as pl
from jax.experimental.pallas import tpu as pltpu
from jax.sharding import PartitionSpec as P

NCT = 4
LOG2E = 1.4426950408889634
DEAD = -1e30
BYTES = 1 << 20
VMEM_LIMIT = 24 << 20
PREPARE_VMEM_LIMIT = 56 << 20

SMEM = pl.BlockSpec(memory_space=pltpu.SMEM)
NT = (((1,), (1,)), ((), ()))
NN = (((1,), (0,)), ((), ()))
TN = (((0,), (0,)), ((), ()))


def dot(a, b, dims):
    return lax.dot_general(a, b, dims, preferred_element_type=jnp.float32)


def swaps_along(size):
    return [
        [(p, p + 1) for p in range(first, size - 1, 2)] for first in (0, 1) if first + 1 < size
    ]


def both_ways(pairs):
    return [(a, b) for a, b in pairs] + [(b, a) for a, b in pairs]


def row_route(swap, col_count):
    return [
        (a * col_count + col, b * col_count + col)
        for a, b in both_ways(swap)
        for col in range(col_count)
    ]


def col_route(swap, row_count, col_count):
    return [
        (row * col_count + a, row * col_count + b)
        for a, b in both_ways(swap)
        for row in range(row_count)
    ]


def partner(at, place, size):
    other = jnp.where(lax.rem(place, 2) == at, place + 1, place - 1)
    return jnp.clip(other, 0, size - 1), (other >= 0) & (other < size)


def table_rows(plan):
    cols = 1
    frames = cols + plan.nc
    flips = frames + plan.nf
    return cols, frames, flips


def table_shape(plan):
    rows = table_rows(plan)[-1] + plan.pairs
    return jax.ShapeDtypeStruct((-(-rows // 8) * 8, plan.hd), jnp.int32)


def prepare_kernel(plan, offsets_ref, counts_ref, q_ref, k_ref, v_ref, *refs):
    table_ref, plane_ref, across_ref, q_out_ref, sems = refs
    hd = plan.hd
    flips, copies = [], []
    for pair in range(plan.pairs):
        hits = jnp.int32(0)
        for slot in range(offsets_ref.shape[2]):
            hits = hits | jnp.abs(offsets_ref[2 * pair, 0, slot])
        flip = jnp.where(hits != 0, 1, 0).astype(jnp.int32)
        flips.append(flip)
        at = pl.ds(pair * hd, hd)
        for kind, near_ref in enumerate((plane_ref, across_ref)):
            head = 2 * pair + (flip if kind == 0 else 1 - flip)
            cols = pl.ds(pl.multiple_of(head * hd, hd), hd)
            targets = [
                (k_ref, near_ref.at[0, :, at]),
                (v_ref, near_ref.at[1, :, at]),
                (q_ref, q_out_ref.at[:, pl.ds((2 * pair + kind) * hd, hd)]),
            ]
            for source, target in targets:
                sem = sems.at[len(copies)]
                copies.append(pltpu.make_async_copy(source.at[:, cols], target, sem))
                copies[-1].start()
    frame, spot = lax.axis_index("frame"), lax.axis_index("tile")
    row, col = lax.div(spot, plan.col_count), lax.rem(spot, plan.col_count)
    entries = [counts_ref[frame, spot]]
    for at in range(plan.nc):
        other, there = partner(at, col, plan.col_count)
        entries.append(jnp.where(there, counts_ref[frame, row * plan.col_count + other], 0))
    for at in range(plan.nf):
        other, there = partner(at, frame, plan.frame_count)
        entries.append(jnp.where(there, counts_ref[other, spot], 0))
    entries += flips
    entries += [jnp.int32(0)] * (table_ref.shape[0] - len(entries))
    for at, entry in enumerate(entries):
        table_ref[at : at + 1, :] = jnp.full((1, hd), entry, jnp.int32)
    for copy in copies:
        copy.wait()


def gather_kernel(plan, table_ref, grad_ref, *refs):
    got_refs, out_ref = refs[:-1], refs[-1]
    section = lax.axis_index("section")
    sections = len(refs)
    flips = table_rows(plan)[-1]
    count = table_ref[0:1, :]
    rows, width, hd = grad_ref.shape[0], out_ref.shape[1], plan.hd
    at_rows = lax.broadcasted_iota(jnp.int32, (rows, hd), 0)
    for k in range(sections):
        holder = lax.rem(section + sections - k, sections)
        live = at_rows + holder * rows < count
        start = pl.multiple_of(holder * rows, rows)
        for pair in range(plan.pairs):
            heads = []
            for head in (2 * pair, 2 * pair + 1):
                at = pl.multiple_of(section * width + head * hd, hd)
                if k == 0:
                    part = grad_ref[:, pl.ds(at, hd)]
                else:
                    part = got_refs[k - 1][:, pl.ds(at, hd)]
                heads.append(jnp.where(live, part.astype(jnp.float32), 0.0))
            for i, part in enumerate(in_order(table_ref, flips + pair, *heads)):
                part = part.astype(out_ref.dtype)
                out_ref[pl.ds(start, rows), pl.ds((2 * pair + i) * hd, hd)] = part


def in_order(table_ref, row, a, b):
    flip = jnp.broadcast_to(table_ref[row : row + 1, :], a.shape) != 0
    return jnp.where(flip, b, a), jnp.where(flip, a, b)


def windows(plan, kv_refs):
    cols, frames, _ = table_rows(plan)
    per_kind = (kv_refs[: 1 + plan.nc], kv_refs[1 + plan.nc :])
    block = 0
    for pair in range(plan.pairs):
        for kind, first in ((0, cols), (1, frames)):
            slots = []
            for at, ref in enumerate(per_kind[kind]):
                row = 0 if at == 0 else first + at - 1
                slots.append((block, ref, pl.ds(pair * plan.hd, plan.hd), row))
                block += 1
            yield pair, kind, pl.ds((2 * pair + kind) * plan.hd, plan.hd), slots


def block_count(plan):
    return plan.pairs * (2 + plan.nc + plan.nf)


def block_weights(plan, table_ref, ref, at, row, q):
    at_rows = lax.broadcasted_iota(jnp.int32, (plan.tile, plan.hd), 0)
    bias = jnp.where(at_rows < table_ref[row : row + 1, :], 0.0, DEAD)
    bias = jnp.concatenate([bias] * (plan.tile // plan.hd), axis=1)
    scores = dot(ref[0, :, at], q, NT) * plan.factor + bias
    top = jnp.max(scores, axis=0, keepdims=True)
    weight = jnp.exp2(scores - top)
    return weight, top, jnp.sum(weight, axis=0, keepdims=True)


def merge(parts):
    top = functools.reduce(jnp.maximum, [log_total for log_total, _ in parts])
    weights = [jnp.exp2(log_total - top) for log_total, _ in parts]
    total = sum(weights)
    mean = sum(w * mean for w, (_, mean) in zip(weights, parts)) / total
    return top + jnp.log(total) * LOG2E, mean


def totals_at(plan, at, pair, kind):
    return pl.ds(4 * at + 2 * kind, 2), pl.ds(pair * plan.tile, plan.tile)


def totals_shape(plan, sets):
    return jax.ShapeDtypeStruct((4 * sets, plan.pairs * plan.tile), jnp.float32)


def totals(parts):
    top = functools.reduce(jnp.maximum, [top for top, _, _ in parts])
    weights = [jnp.exp2(part_top - top) for part_top, _, _ in parts]
    total = sum(w * total for w, (_, total, _) in zip(weights, parts))
    cross = sum(w * cross for w, (_, _, cross) in zip(weights, parts))
    return jnp.concatenate([top + jnp.log(total) * LOG2E, cross / total], axis=0)


def own_kernel(plan, table_ref, q_ref, grad_ref, *refs):
    *kv_refs, weight_ref, top_ref, slope_ref, total_ref = refs
    for pair, kind, cols, slots in windows(plan, kv_refs):
        parts = []
        for block, ref, at, row in slots:
            weight, top, total = block_weights(plan, table_ref, ref, at, row, q_ref[:, cols])
            slope = dot(ref[1, :, at], grad_ref[:, cols], NT)
            weight_ref[block] = weight
            slope_ref[block] = slope
            top_ref[block : block + 1, :] = top
            parts.append((top, total, jnp.sum(weight * slope, axis=0, keepdims=True)))
        total_ref[totals_at(plan, 0, pair, kind)] = totals(parts)


def order_kernel(plan, table_ref, q_ref, out_ref):
    hd = plan.hd
    flips = table_rows(plan)[-1]
    for pair in range(plan.pairs):
        cols = [pl.ds((2 * pair + i) * hd, hd) for i in (0, 1)]
        heads = [q_ref[:, at].astype(jnp.float32) for at in cols]
        for at, part in zip(cols, in_order(table_ref, flips + pair, *heads)):
            out_ref[:, at] = part.astype(out_ref.dtype)


def far_weights_kernel(plan, table_ref, q_ref, *refs):
    *kv_refs, weight_ref, top_ref, sum_ref = refs
    for pair, kind, cols, slots in windows(plan, kv_refs):
        for block, ref, at, row in slots:
            weight, top, total = block_weights(plan, table_ref, ref, at, row, q_ref[:, cols])
            weight_ref[block] = weight
            top_ref[block : block + 1, :] = top
            sum_ref[block : block + 1, :] = total


def far_totals_kernel(plan, weight_ref, top_ref, sum_ref, own_ref, grad_ref, *refs):
    *kv_refs, slope_ref, total_ref = refs
    total_ref[0:4, :] = own_ref[...]
    for pair, kind, cols, slots in windows(plan, kv_refs):
        parts = []
        for block, ref, at, _ in slots:
            slope = dot(ref[1, :, at], grad_ref[:, cols], NT)
            slope_ref[block] = slope
            cross = jnp.sum(weight_ref[block] * slope, axis=0, keepdims=True)
            parts.append((top_ref[block : block + 1, :], sum_ref[block : block + 1, :], cross))
        total_ref[totals_at(plan, 1, pair, kind)] = totals(parts)


def head_grads(plan, sets, total_refs, kv_refs):
    for pair, kind, cols, slots in windows(plan, kv_refs):
        log_totals, row_dots = [], []
        for places in plan.totals_of:
            parts = []
            for ref, place in places:
                part = total_refs[ref][totals_at(plan, place, pair, kind)]
                parts.append((part[0:1], part[1:2]))
            log_total, row_dot = merge(parts)
            log_totals.append(log_total)
            row_dots.append(row_dot)

        def tile_grads(block, log_totals=log_totals, row_dots=row_dots):
            softmax, grad_scores = [], []
            for (weight_ref, top_ref, slope_ref, _, _), log_total, row_dot in zip(
                sets, log_totals, row_dots
            ):
                scale = jnp.exp2(top_ref[block : block + 1, :] - log_total)
                part = weight_ref[block] * scale
                softmax.append(part.astype(jnp.bfloat16))
                grad_scores.append((part * (slope_ref[block] - row_dot)).astype(jnp.bfloat16))
            return jnp.concatenate(softmax, axis=1), jnp.concatenate(grad_scores, axis=1)

        q = jnp.concatenate([q_ref[:, cols] for _, _, _, q_ref, _ in sets], axis=0)
        grad = jnp.concatenate([grad_ref[:, cols] for _, _, _, _, grad_ref in sets], axis=0)
        yield kind, cols, q, grad, slots, tile_grads


def first_grads_kernel(plan, *refs):
    refs = list(refs)
    take = lambda n: [refs.pop(0) for _ in range(n)]
    sets = [take(5) for _ in range(1 + plan.nr)]
    kv_refs, total_refs = take(2 + plan.nc + plan.nf), take(plan.n_totals)
    dq_refs = take(1 + plan.nr)
    for kind, cols, q, grad, slots, tile_grads in head_grads(plan, sets, total_refs, kv_refs):
        query_grad = None
        for slot, (block, ref, at, _) in enumerate(slots):
            softmax, grad_scores = tile_grads(block)
            term = dot(ref[0, :, at], grad_scores, TN)
            query_grad = term if query_grad is None else query_grad + term
            if kind == 0 and slot > 0:
                dk = dot(grad_scores, q, NN) * plan.scale
                refs[slot - 1][0, :, at] = dk.astype(jnp.bfloat16)
                refs[slot - 1][1, :, at] = dot(softmax, grad, NN).astype(jnp.bfloat16)
        query_grad = jnp.transpose(query_grad * plan.scale)
        for at, ref in enumerate(dq_refs):
            rows = query_grad[at * plan.tile : (at + 1) * plan.tile]
            ref[:, cols] = rows.astype(ref.dtype)


def last_grads_kernel(plan, *refs):
    refs = list(refs)
    take = lambda n: [refs.pop(0) for _ in range(n)]
    sets = [take(5) for _ in range(1 + plan.nr)]
    kv_refs, total_refs = take(2 + plan.nc + plan.nf), take(plan.n_totals)
    own_refs = take(2)
    for kind, cols, q, grad, slots, tile_grads in head_grads(plan, sets, total_refs, kv_refs):
        for slot, (block, ref, at, _) in enumerate(slots if kind else slots[:1]):
            softmax, grad_scores = tile_grads(block)
            dk = dot(grad_scores, q, NN) * plan.scale
            dv = dot(softmax, grad, NN)
            for i, out in enumerate((dk, dv)):
                if slot == 0:
                    own_refs[i][:, cols] = out
                else:
                    refs[slot - 1][i, :, at] = out.astype(jnp.bfloat16)


def add_query_kernel(plan, table_ref, *refs):
    *refs, out_ref = refs
    flips, hd = table_rows(plan)[-1], plan.hd
    for pair in range(plan.pairs):
        cols = [pl.ds((2 * pair + kind) * hd, hd) for kind in (0, 1)]
        parts = [sum(ref[:, at].astype(jnp.float32) for ref in refs) for at in cols]
        for at, head in zip(cols, in_order(table_ref, flips + pair, *parts)):
            out_ref[:, at] = head.astype(out_ref.dtype)


def add_key_kernel(plan, table_ref, *refs):
    refs = list(refs)
    take = lambda n: [refs.pop(0) for _ in range(n)]
    flips, hd = table_rows(plan)[-1], plan.hd
    own, near = take(2), (take(plan.nc), take(plan.nf))
    for pair in range(plan.pairs):
        cols = [pl.ds((2 * pair + kind) * hd, hd) for kind in (0, 1)]
        near_at = pl.ds(pair * hd, hd)
        for i, out_ref in enumerate(refs):
            parts = []
            for kind in (0, 1):
                total = own[i][:, cols[kind]]
                for ref in near[kind]:
                    total = total + ref[i, :, near_at].astype(jnp.float32)
                parts.append(total)
            for at, head in zip(cols, in_order(table_ref, flips + pair, *parts)):
                out_ref[:, at] = head.astype(out_ref.dtype)


class Plan:
    pass


def params():
    return pltpu.CompilerParams(vmem_limit_bytes=VMEM_LIMIT)


def local(queries, key_rows, value_rows, grad_rows, offsets, counts):
    q, k, v, grad = queries[0, 0], key_rows[0, 0], value_rows[0, 0], grad_rows[0, 0]
    tile, width = q.shape
    heads = offsets.shape[0]
    pairs = heads // 2
    hd = width // heads
    sections = lax.axis_size("section")
    frame_count = lax.axis_size("frame")
    col_count = NCT
    row_count = lax.axis_size("tile") // col_count

    plan = Plan()
    plan.tile, plan.hd, plan.col_count = tile, hd, col_count
    plan.scale = 1.0 / math.sqrt(hd)
    plan.factor = plan.scale * LOG2E
    row_swaps = swaps_along(row_count)
    col_swaps = swaps_along(col_count)
    frame_swaps = swaps_along(frame_count)
    plan.nr, plan.nc, plan.nf = len(row_swaps), len(col_swaps), len(frame_swaps)
    plan.frame_count = frame_count
    row_routes = [row_route(swap, col_count) for swap in row_swaps]
    col_routes = [col_route(swap, row_count, col_count) for swap in col_swaps]
    frame_routes = [both_ways(swap) for swap in frame_swaps]

    def from_rows(x):
        return [lax.ppermute(x, "tile", route) for route in row_routes]

    vm = pl.BlockSpec(memory_space=pltpu.VMEM)
    plan.row_count = row_count

    plan.pairs = pairs

    def call(kernel, name, out_shape, flops, *operands, nbytes=BYTES):
        return pl.pallas_call(
            functools.partial(kernel, plan),
            out_shape=out_shape,
            in_specs=[vm] * len(operands),
            out_specs=[vm] * len(out_shape),
            compiler_params=params(),
            cost_estimate=pl.CostEstimate(
                flops=flops, bytes_accessed=nbytes, transcendentals=0
            ),
            name=name,
        )(*operands)

    low = jax.ShapeDtypeStruct((tile, width), jnp.bfloat16)
    wide = jax.ShapeDtypeStruct((tile, width), jnp.float32)
    packed = jax.ShapeDtypeStruct((2, tile, pairs * hd), jnp.bfloat16)
    blocks = block_count(plan)
    block_shape = jax.ShapeDtypeStruct((blocks, tile, tile), jnp.float32)
    rows_shape = jax.ShapeDtypeStruct((-(-blocks // 8) * 8, tile), jnp.float32)

    got = []
    for shift in range(1, sections):
        route = [(i, (i + shift) % sections) for i in range(sections)]
        got.append(lax.ppermute(grad, "section", route))
    far_q_raw = from_rows(q)

    hbm = pl.BlockSpec(memory_space=pl.ANY)
    table, plane_kv, across_kv, own_q = pl.pallas_call(
        functools.partial(prepare_kernel, plan),
        out_shape=[table_shape(plan), packed, packed, low],
        in_specs=[SMEM] * 2 + [hbm] * 3,
        out_specs=[vm] * 4,
        scratch_shapes=[pltpu.SemaphoreType.DMA((6 * pairs,))],
        compiler_params=pltpu.CompilerParams(vmem_limit_bytes=PREPARE_VMEM_LIMIT),
        cost_estimate=pl.CostEstimate(flops=0, bytes_accessed=0, transcendentals=0),
        name="prepare",
    )(jnp.transpose(offsets, (0, 2, 1)), counts, q, k, v)

    (own_grad,) = call(gather_kernel, "gather_grad", [low], 0, table, grad, *got)

    near_plane = [lax.ppermute(plane_kv, "tile", route) for route in col_routes]
    near_across = [lax.ppermute(across_kv, "frame", route) for route in frame_routes]
    kv = [plane_kv, *near_plane, across_kv, *near_across]
    far_grad = from_rows(own_grad)

    matmul = 2 * blocks * tile * tile * hd
    far_q = [call(order_kernel, "order_queries", [low], 0, table, raw)[0] for raw in far_q_raw]
    table, *far_q = lax.optimization_barrier((table, *far_q))
    own_weight, own_top, own_slope, own_total = call(
        own_kernel,
        "own_rows",
        [block_shape, rows_shape, block_shape, totals_shape(plan, 1)],
        2 * matmul,
        *(table, own_q, own_grad, *kv),
    )
    sets = [(own_weight, own_top, own_slope, own_q, own_grad)]
    far_totals = []
    for queries, far in zip(far_q, far_grad):
        weight, top, total = call(
            far_weights_kernel,
            "far_weights",
            [block_shape, rows_shape, rows_shape],
            matmul,
            *(table, queries, *kv),
        )
        slope, total = call(
            far_totals_kernel,
            "far_totals",
            [block_shape, totals_shape(plan, 2)],
            matmul,
            *(weight, top, total, own_total, far, *kv),
        )
        sets.append((weight, top, slope, queries, far))
        far_totals.append(total)
    shared, plan.totals_of = share_totals(own_total, far_totals, row_routes)
    plan.n_totals = len(shared)

    nq = 1 + plan.nr
    operands = [ref for refs in sets for ref in refs] + kv + shared
    outs = call(
        first_grads_kernel,
        "first_grads",
        [wide] + [low] * plan.nr + [packed] * plan.nc,
        2 * nq * matmul,
        *operands,
    )
    own_dq, far_dq, plane_out = outs[0], outs[1:nq], outs[nq:]
    back = [lax.ppermute(x, "tile", r) for x, r in zip(far_dq, row_routes)]
    back_plane = [lax.ppermute(x, "tile", r) for x, r in zip(plane_out, col_routes)]
    operands[-1], _ = lax.optimization_barrier((operands[-1], own_dq))
    own_dk, own_dv, *across_out = call(
        last_grads_kernel,
        "last_grads",
        [wide] * 2 + [packed] * plan.nf,
        nq * matmul,
        *operands,
    )
    back_across = [lax.ppermute(x, "frame", r) for x, r in zip(across_out, frame_routes)]
    (dq,) = call(add_query_kernel, "add_query", [low], 0, table, own_dq, *back)
    dk, dv = call(
        add_key_kernel,
        "add_key",
        [low] * 2,
        0,
        *(table, own_dk, own_dv, *back_plane, *back_across),
    )
    return dq[None, None], dk[None, None], dv[None, None]


def share_totals(own, far, row_routes):
    if len(far) == 0:
        return [own], [[(0, 0)]]
    if len(far) == 1:
        back = lax.ppermute(far[0], "tile", row_routes[0])
        return [far[0], back], [[(0, 0), (1, 1)], [(0, 1), (1, 0)]]
    terms = [own]
    for part, route in zip(far, row_routes):
        term = lax.ppermute(part[4:], "tile", route)
        there = lax.ppermute(jnp.ones((8, 128), jnp.float32), "tile", route)[0, 0] > 0
        logs = jnp.array([1, 0, 1, 0], jnp.float32)[:, None]
        terms.append(jnp.where(there, term, DEAD * logs))
    merged = []
    for kind in (0, 1):
        merged += merge([(t[2 * kind], t[2 * kind + 1]) for t in terms])
    total = jnp.stack(merged)
    shared = [total] + [lax.ppermute(total, "tile", route) for route in row_routes]
    return shared, [[(at, 0)] for at in range(len(shared))]


def solution(mesh):
    return jax.shard_map(
        local,
        mesh=mesh,
        in_specs=(
            P("frame", "tile", None, "section"),
            P("frame", "tile", None, "section"),
            P("frame", "tile", None, "section"),
            P("frame", "tile", "section", None),
            P("section", None, None),
            P(),
        ),
        out_specs=(
            P("frame", "tile", None, "section"),
            P("frame", "tile", None, "section"),
            P("frame", "tile", None, "section"),
        ),
        check_vma=False,
    )
```

```python
import functools
import math

import jax
import jax.numpy as jnp
from jax import lax
from jax.experimental import pallas as pl
from jax.experimental.pallas import tpu as pltpu
from jax.sharding import PartitionSpec as P

NCT = 4
LOG2E = 1.4426950408889634
DEAD = -1e30
BYTES = 1 << 20
VMEM_LIMIT = 24 << 20
PREPARE_VMEM_LIMIT = 56 << 20

SMEM = pl.BlockSpec(memory_space=pltpu.SMEM)
NT = (((1,), (1,)), ((), ()))
NN = (((1,), (0,)), ((), ()))
TN = (((0,), (0,)), ((), ()))


def dot(a, b, dims):
    return lax.dot_general(a, b, dims, preferred_element_type=jnp.float32)


def swaps_along(size):
    return [
        [(p, p + 1) for p in range(first, size - 1, 2)] for first in (0, 1) if first + 1 < size
    ]


def both_ways(pairs):
    return [(a, b) for a, b in pairs] + [(b, a) for a, b in pairs]


def row_route(swap, col_count):
    return [
        (a * col_count + col, b * col_count + col)
        for a, b in both_ways(swap)
        for col in range(col_count)
    ]


def col_route(swap, row_count, col_count):
    return [
        (row * col_count + a, row * col_count + b)
        for a, b in both_ways(swap)
        for row in range(row_count)
    ]


def partner(at, place, size):
    other = jnp.where(lax.rem(place, 2) == at, place + 1, place - 1)
    return jnp.clip(other, 0, size - 1), (other >= 0) & (other < size)


def table_rows(plan):
    cols = 1
    frames = cols + plan.nc
    flips = frames + plan.nf
    return cols, frames, flips


def table_shape(plan):
    rows = table_rows(plan)[-1] + plan.pairs
    return jax.ShapeDtypeStruct((-(-rows // 8) * 8, plan.hd), jnp.int32)


def prepare_kernel(plan, offsets_ref, counts_ref, q_ref, k_ref, v_ref, *refs):
    table_ref, plane_ref, across_ref, q_out_ref, sems = refs
    hd = plan.hd
    flips, copies = [], []
    for pair in range(plan.pairs):
        hits = jnp.int32(0)
        for slot in range(offsets_ref.shape[2]):
            hits = hits | jnp.abs(offsets_ref[2 * pair, 0, slot])
        flip = jnp.where(hits != 0, 1, 0).astype(jnp.int32)
        flips.append(flip)
        at = pl.ds(pair * hd, hd)
        for kind, near_ref in enumerate((plane_ref, across_ref)):
            head = 2 * pair + (flip if kind == 0 else 1 - flip)
            cols = pl.ds(pl.multiple_of(head * hd, hd), hd)
            targets = [
                (k_ref, near_ref.at[0, :, at]),
                (v_ref, near_ref.at[1, :, at]),
                (q_ref, q_out_ref.at[:, pl.ds((2 * pair + kind) * hd, hd)]),
            ]
            for source, target in targets:
                sem = sems.at[len(copies)]
                copies.append(pltpu.make_async_copy(source.at[:, cols], target, sem))
                copies[-1].start()
    frame, spot = lax.axis_index("frame"), lax.axis_index("tile")
    row, col = lax.div(spot, plan.col_count), lax.rem(spot, plan.col_count)
    entries = [counts_ref[frame, spot]]
    for at in range(plan.nc):
        other, there = partner(at, col, plan.col_count)
        entries.append(jnp.where(there, counts_ref[frame, row * plan.col_count + other], 0))
    for at in range(plan.nf):
        other, there = partner(at, frame, plan.frame_count)
        entries.append(jnp.where(there, counts_ref[other, spot], 0))
    entries += flips
    entries += [jnp.int32(0)] * (table_ref.shape[0] - len(entries))
    for at, entry in enumerate(entries):
        table_ref[at : at + 1, :] = jnp.full((1, hd), entry, jnp.int32)
    for copy in copies:
        copy.wait()


def gather_kernel(plan, table_ref, grad_ref, *refs):
    got_refs, out_ref = refs[:-1], refs[-1]
    section = lax.axis_index("section")
    sections = len(refs)
    flips = table_rows(plan)[-1]
    count = table_ref[0:1, :]
    rows, width, hd = grad_ref.shape[0], out_ref.shape[1], plan.hd
    at_rows = lax.broadcasted_iota(jnp.int32, (rows, hd), 0)
    for k in range(sections):
        holder = lax.rem(section + sections - k, sections)
        live = at_rows + holder * rows < count
        start = pl.multiple_of(holder * rows, rows)
        for pair in range(plan.pairs):
            heads = []
            for head in (2 * pair, 2 * pair + 1):
                at = pl.multiple_of(section * width + head * hd, hd)
                if k == 0:
                    part = grad_ref[:, pl.ds(at, hd)]
                else:
                    part = got_refs[k - 1][:, pl.ds(at, hd)]
                heads.append(jnp.where(live, part.astype(jnp.float32), 0.0))
            for i, part in enumerate(in_order(table_ref, flips + pair, *heads)):
                part = part.astype(out_ref.dtype)
                out_ref[pl.ds(start, rows), pl.ds((2 * pair + i) * hd, hd)] = part


def in_order(table_ref, row, a, b):
    flip = jnp.broadcast_to(table_ref[row : row + 1, :], a.shape) != 0
    return jnp.where(flip, b, a), jnp.where(flip, a, b)


def windows(plan, kv_refs):
    cols, frames, _ = table_rows(plan)
    per_kind = (kv_refs[: 1 + plan.nc], kv_refs[1 + plan.nc :])
    block = 0
    for pair in range(plan.pairs):
        for kind, first in ((0, cols), (1, frames)):
            slots = []
            for at, ref in enumerate(per_kind[kind]):
                row = 0 if at == 0 else first + at - 1
                slots.append((block, ref, pl.ds(pair * plan.hd, plan.hd), row))
                block += 1
            yield pair, kind, pl.ds((2 * pair + kind) * plan.hd, plan.hd), slots


def block_count(plan):
    return plan.pairs * (2 + plan.nc + plan.nf)


def block_weights(plan, table_ref, ref, at, row, q):
    at_rows = lax.broadcasted_iota(jnp.int32, (plan.tile, plan.hd), 0)
    bias = jnp.where(at_rows < table_ref[row : row + 1, :], 0.0, DEAD)
    bias = jnp.concatenate([bias] * (plan.tile // plan.hd), axis=1)
    scores = dot(ref[0, :, at], q, NT) * plan.factor + bias
    top = jnp.max(scores, axis=0, keepdims=True)
    weight = jnp.exp2(scores - top)
    return weight, top, jnp.sum(weight, axis=0, keepdims=True)


def merge(parts):
    top = functools.reduce(jnp.maximum, [log_total for log_total, _ in parts])
    weights = [jnp.exp2(log_total - top) for log_total, _ in parts]
    total = sum(weights)
    mean = sum(w * mean for w, (_, mean) in zip(weights, parts)) / total
    return top + jnp.log(total) * LOG2E, mean


def totals_at(plan, at, pair, kind):
    return pl.ds(4 * at + 2 * kind, 2), pl.ds(pair * plan.tile, plan.tile)


def totals_shape(plan, sets):
    return jax.ShapeDtypeStruct((4 * sets, plan.pairs * plan.tile), jnp.float32)


def totals(parts):
    top = functools.reduce(jnp.maximum, [top for top, _, _ in parts])
    weights = [jnp.exp2(part_top - top) for part_top, _, _ in parts]
    total = sum(w * total for w, (_, total, _) in zip(weights, parts))
    cross = sum(w * cross for w, (_, _, cross) in zip(weights, parts))
    return jnp.concatenate([top + jnp.log(total) * LOG2E, cross / total], axis=0)


def own_kernel(plan, table_ref, q_ref, grad_ref, *refs):
    *kv_refs, weight_ref, top_ref, slope_ref, total_ref = refs
    for pair, kind, cols, slots in windows(plan, kv_refs):
        parts = []
        for block, ref, at, row in slots:
            weight, top, total = block_weights(plan, table_ref, ref, at, row, q_ref[:, cols])
            slope = dot(ref[1, :, at], grad_ref[:, cols], NT)
            weight_ref[block] = weight
            slope_ref[block] = slope
            top_ref[block : block + 1, :] = top
            parts.append((top, total, jnp.sum(weight * slope, axis=0, keepdims=True)))
        total_ref[totals_at(plan, 0, pair, kind)] = totals(parts)


def order_kernel(plan, table_ref, q_ref, out_ref):
    hd = plan.hd
    flips = table_rows(plan)[-1]
    for pair in range(plan.pairs):
        cols = [pl.ds((2 * pair + i) * hd, hd) for i in (0, 1)]
        heads = [q_ref[:, at].astype(jnp.float32) for at in cols]
        for at, part in zip(cols, in_order(table_ref, flips + pair, *heads)):
            out_ref[:, at] = part.astype(out_ref.dtype)


def far_weights_kernel(plan, table_ref, q_ref, *refs):
    *kv_refs, weight_ref, top_ref, sum_ref = refs
    for pair, kind, cols, slots in windows(plan, kv_refs):
        for block, ref, at, row in slots:
            weight, top, total = block_weights(plan, table_ref, ref, at, row, q_ref[:, cols])
            weight_ref[block] = weight
            top_ref[block : block + 1, :] = top
            sum_ref[block : block + 1, :] = total


def far_totals_kernel(plan, weight_ref, top_ref, sum_ref, own_ref, grad_ref, *refs):
    *kv_refs, slope_ref, total_ref = refs
    total_ref[0:4, :] = own_ref[...]
    for pair, kind, cols, slots in windows(plan, kv_refs):
        parts = []
        for block, ref, at, _ in slots:
            slope = dot(ref[1, :, at], grad_ref[:, cols], NT)
            slope_ref[block] = slope
            cross = jnp.sum(weight_ref[block] * slope, axis=0, keepdims=True)
            parts.append((top_ref[block : block + 1, :], sum_ref[block : block + 1, :], cross))
        total_ref[totals_at(plan, 1, pair, kind)] = totals(parts)


def head_grads(plan, sets, total_refs, kv_refs):
    for pair, kind, cols, slots in windows(plan, kv_refs):
        log_totals, row_dots = [], []
        for places in plan.totals_of:
            parts = []
            for ref, place in places:
                part = total_refs[ref][totals_at(plan, place, pair, kind)]
                parts.append((part[0:1], part[1:2]))
            log_total, row_dot = merge(parts)
            log_totals.append(log_total)
            row_dots.append(row_dot)

        def tile_grads(block, places, log_totals=log_totals, row_dots=row_dots):
            softmax, grad_scores = [], []
            for place in places:
                weight_ref, top_ref, slope_ref, _, _ = sets[place]
                scale = jnp.exp2(top_ref[block : block + 1, :] - log_totals[place])
                part = weight_ref[block] * scale
                softmax.append(part.astype(jnp.bfloat16))
                part = part * (slope_ref[block] - row_dots[place])
                grad_scores.append(part.astype(jnp.bfloat16))
            return jnp.concatenate(softmax, axis=1), jnp.concatenate(grad_scores, axis=1)

        q = jnp.concatenate([q_ref[:, cols] for _, _, _, q_ref, _ in sets], axis=0)
        grad = jnp.concatenate([grad_ref[:, cols] for _, _, _, _, grad_ref in sets], axis=0)
        yield kind, cols, q, grad, slots, tile_grads


def add(total, term):
    return term if total is None else total + term


def first_grads_kernel(plan, *refs):
    refs = list(refs)
    take = lambda n: [refs.pop(0) for _ in range(n)]
    sets = [take(5) for _ in range(1 + plan.nr)]
    kv_refs, total_refs = take(2 + plan.nc + plan.nf), take(plan.n_totals)
    dq_refs = take(plan.nr)
    tile = plan.tile
    everyone, far = range(1 + plan.nr), range(1, 1 + plan.nr)
    for kind, cols, q, grad, slots, tile_grads in head_grads(plan, sets, total_refs, kv_refs):
        query_grad = None
        for slot, (block, ref, at, _) in enumerate(slots):
            near = kind == 0 and slot > 0
            if not near and not dq_refs:
                continue
            softmax, grad_scores = tile_grads(block, everyone if near else far)
            if dq_refs:
                far_scores = grad_scores[:, tile:] if near else grad_scores
                query_grad = add(query_grad, dot(ref[0, :, at], far_scores, TN))
            if near:
                dk = dot(grad_scores, q, NN) * plan.scale
                refs[slot - 1][0, :, at] = dk.astype(jnp.bfloat16)
                refs[slot - 1][1, :, at] = dot(softmax, grad, NN).astype(jnp.bfloat16)
        if dq_refs:
            query_grad = jnp.transpose(query_grad * plan.scale)
        for at, ref in enumerate(dq_refs):
            ref[:, cols] = query_grad[at * tile : (at + 1) * tile].astype(ref.dtype)


def last_grads_kernel(plan, *refs):
    refs = list(refs)
    take = lambda n: [refs.pop(0) for _ in range(n)]
    sets = [take(5) for _ in range(1 + plan.nr)]
    kv_refs, total_refs = take(2 + plan.nc + plan.nf), take(plan.n_totals)
    dq_ref, *own_refs = take(3)
    tile = plan.tile
    everyone, own = range(1 + plan.nr), range(1)
    for kind, cols, q, grad, slots, tile_grads in head_grads(plan, sets, total_refs, kv_refs):
        query_grad = None
        for slot, (block, ref, at, _) in enumerate(slots):
            near = kind == 0 and slot > 0
            softmax, grad_scores = tile_grads(block, own if near else everyone)
            query_grad = add(query_grad, dot(ref[0, :, at], grad_scores[:, :tile], TN))
            if near:
                continue
            dk = dot(grad_scores, q, NN) * plan.scale
            dv = dot(softmax, grad, NN)
            for i, out in enumerate((dk, dv)):
                if slot == 0:
                    own_refs[i][:, cols] = out
                else:
                    refs[slot - 1][i, :, at] = out.astype(jnp.bfloat16)
        dq_ref[:, cols] = jnp.transpose(query_grad * plan.scale)


def add_query_kernel(plan, table_ref, *refs):
    *refs, out_ref = refs
    flips, hd = table_rows(plan)[-1], plan.hd
    for pair in range(plan.pairs):
        cols = [pl.ds((2 * pair + kind) * hd, hd) for kind in (0, 1)]
        parts = [sum(ref[:, at].astype(jnp.float32) for ref in refs) for at in cols]
        for at, head in zip(cols, in_order(table_ref, flips + pair, *parts)):
            out_ref[:, at] = head.astype(out_ref.dtype)


def add_key_kernel(plan, table_ref, *refs):
    refs = list(refs)
    take = lambda n: [refs.pop(0) for _ in range(n)]
    flips, hd = table_rows(plan)[-1], plan.hd
    own, near = take(2), (take(plan.nc), take(plan.nf))
    for pair in range(plan.pairs):
        cols = [pl.ds((2 * pair + kind) * hd, hd) for kind in (0, 1)]
        near_at = pl.ds(pair * hd, hd)
        for i, out_ref in enumerate(refs):
            parts = []
            for kind in (0, 1):
                total = own[i][:, cols[kind]]
                for ref in near[kind]:
                    total = total + ref[i, :, near_at].astype(jnp.float32)
                parts.append(total)
            for at, head in zip(cols, in_order(table_ref, flips + pair, *parts)):
                out_ref[:, at] = head.astype(out_ref.dtype)


class Plan:
    pass


def params():
    return pltpu.CompilerParams(vmem_limit_bytes=VMEM_LIMIT)


def local(queries, key_rows, value_rows, grad_rows, offsets, counts):
    q, k, v, grad = queries[0, 0], key_rows[0, 0], value_rows[0, 0], grad_rows[0, 0]
    tile, width = q.shape
    heads = offsets.shape[0]
    pairs = heads // 2
    hd = width // heads
    sections = lax.axis_size("section")
    frame_count = lax.axis_size("frame")
    col_count = NCT
    row_count = lax.axis_size("tile") // col_count

    plan = Plan()
    plan.tile, plan.hd, plan.col_count = tile, hd, col_count
    plan.scale = 1.0 / math.sqrt(hd)
    plan.factor = plan.scale * LOG2E
    row_swaps = swaps_along(row_count)
    col_swaps = swaps_along(col_count)
    frame_swaps = swaps_along(frame_count)
    plan.nr, plan.nc, plan.nf = len(row_swaps), len(col_swaps), len(frame_swaps)
    plan.frame_count = frame_count
    row_routes = [row_route(swap, col_count) for swap in row_swaps]
    col_routes = [col_route(swap, row_count, col_count) for swap in col_swaps]
    frame_routes = [both_ways(swap) for swap in frame_swaps]

    def from_rows(x):
        return [lax.ppermute(x, "tile", route) for route in row_routes]

    vm = pl.BlockSpec(memory_space=pltpu.VMEM)
    plan.row_count = row_count

    plan.pairs = pairs

    def call(kernel, name, out_shape, flops, *operands, nbytes=BYTES):
        return pl.pallas_call(
            functools.partial(kernel, plan),
            out_shape=out_shape,
            in_specs=[vm] * len(operands),
            out_specs=[vm] * len(out_shape),
            compiler_params=params(),
            cost_estimate=pl.CostEstimate(
                flops=flops, bytes_accessed=nbytes, transcendentals=0
            ),
            name=name,
        )(*operands)

    low = jax.ShapeDtypeStruct((tile, width), jnp.bfloat16)
    wide = jax.ShapeDtypeStruct((tile, width), jnp.float32)
    packed = jax.ShapeDtypeStruct((2, tile, pairs * hd), jnp.bfloat16)
    blocks = block_count(plan)
    block_shape = jax.ShapeDtypeStruct((blocks, tile, tile), jnp.float32)
    rows_shape = jax.ShapeDtypeStruct((-(-blocks // 8) * 8, tile), jnp.float32)

    got = []
    for shift in range(1, sections):
        route = [(i, (i + shift) % sections) for i in range(sections)]
        got.append(lax.ppermute(grad, "section", route))
    far_q_raw = from_rows(q)

    hbm = pl.BlockSpec(memory_space=pl.ANY)
    table, plane_kv, across_kv, own_q = pl.pallas_call(
        functools.partial(prepare_kernel, plan),
        out_shape=[table_shape(plan), packed, packed, low],
        in_specs=[SMEM] * 2 + [hbm] * 3,
        out_specs=[vm] * 4,
        scratch_shapes=[pltpu.SemaphoreType.DMA((6 * pairs,))],
        compiler_params=pltpu.CompilerParams(vmem_limit_bytes=PREPARE_VMEM_LIMIT),
        cost_estimate=pl.CostEstimate(flops=0, bytes_accessed=0, transcendentals=0),
        name="prepare",
    )(jnp.transpose(offsets, (0, 2, 1)), counts, q, k, v)

    (own_grad,) = call(gather_kernel, "gather_grad", [low], 0, table, grad, *got)

    near_plane = [lax.ppermute(plane_kv, "tile", route) for route in col_routes]
    near_across = [lax.ppermute(across_kv, "frame", route) for route in frame_routes]
    kv = [plane_kv, *near_plane, across_kv, *near_across]
    far_grad = from_rows(own_grad)

    matmul = 2 * blocks * tile * tile * hd
    far_q = [call(order_kernel, "order_queries", [low], 0, table, raw)[0] for raw in far_q_raw]
    table, *far_q = lax.optimization_barrier((table, *far_q))
    own_weight, own_top, own_slope, own_total = call(
        own_kernel,
        "own_rows",
        [block_shape, rows_shape, block_shape, totals_shape(plan, 1)],
        2 * matmul,
        *(table, own_q, own_grad, *kv),
    )
    sets = [(own_weight, own_top, own_slope, own_q, own_grad)]
    far_totals = []
    for queries, far in zip(far_q, far_grad):
        weight, top, total = call(
            far_weights_kernel,
            "far_weights",
            [block_shape, rows_shape, rows_shape],
            matmul,
            *(table, queries, *kv),
        )
        slope, total = call(
            far_totals_kernel,
            "far_totals",
            [block_shape, totals_shape(plan, 2)],
            matmul,
            *(weight, top, total, own_total, far, *kv),
        )
        sets.append((weight, top, slope, queries, far))
        far_totals.append(total)
    shared, plan.totals_of = share_totals(own_total, far_totals, row_routes)
    plan.n_totals = len(shared)

    nq = 1 + plan.nr
    operands = [ref for refs in sets for ref in refs] + kv + shared
    outs = call(
        first_grads_kernel,
        "first_grads",
        [low] * plan.nr + [packed] * plan.nc,
        2 * nq * matmul,
        *operands,
    )
    far_dq, plane_out = outs[: plan.nr], outs[plan.nr :]
    back = [lax.ppermute(x, "tile", r) for x, r in zip(far_dq, row_routes)]
    back_plane = [lax.ppermute(x, "tile", r) for x, r in zip(plane_out, col_routes)]
    own_dq, own_dk, own_dv, *across_out = call(
        last_grads_kernel,
        "last_grads",
        [wide] * 3 + [packed] * plan.nf,
        nq * matmul,
        *operands,
    )
    back_across = [lax.ppermute(x, "frame", r) for x, r in zip(across_out, frame_routes)]
    (dq,) = call(add_query_kernel, "add_query", [low], 0, table, own_dq, *back)
    dk, dv = call(
        add_key_kernel,
        "add_key",
        [low] * 2,
        0,
        *(table, own_dk, own_dv, *back_plane, *back_across),
    )
    return dq[None, None], dk[None, None], dv[None, None]


def share_totals(own, far, row_routes):
    if len(far) == 0:
        return [own], [[(0, 0)]]
    if len(far) == 1:
        back = lax.ppermute(far[0], "tile", row_routes[0])
        return [far[0], back], [[(0, 0), (1, 1)], [(0, 1), (1, 0)]]
    terms = [own]
    for part, route in zip(far, row_routes):
        term = lax.ppermute(part[4:], "tile", route)
        there = lax.ppermute(jnp.ones((8, 128), jnp.float32), "tile", route)[0, 0] > 0
        logs = jnp.array([1, 0, 1, 0], jnp.float32)[:, None]
        terms.append(jnp.where(there, term, DEAD * logs))
    merged = []
    for kind in (0, 1):
        merged += merge([(t[2 * kind], t[2 * kind + 1]) for t in terms])
    total = jnp.stack(merged)
    shared = [total] + [lax.ppermute(total, "tile", route) for route in row_routes]
    return shared, [[(at, 0)] for at in range(len(shared))]


def solution(mesh):
    return jax.shard_map(
        local,
        mesh=mesh,
        in_specs=(
            P("frame", "tile", None, "section"),
            P("frame", "tile", None, "section"),
            P("frame", "tile", None, "section"),
            P("frame", "tile", "section", None),
            P("section", None, None),
            P(),
        ),
        out_specs=(
            P("frame", "tile", None, "section"),
            P("frame", "tile", None, "section"),
            P("frame", "tile", None, "section"),
        ),
        check_vma=False,
    )
```

```python
import functools
import math

import jax
import jax.numpy as jnp
from jax import lax
from jax.experimental import pallas as pl
from jax.experimental.pallas import tpu as pltpu
from jax.sharding import PartitionSpec as P

NCT = 4
LOG2E = 1.4426950408889634
DEAD = -1e30
BYTES = 1 << 20
VMEM_LIMIT = 24 << 20
PREPARE_VMEM_LIMIT = 56 << 20

SMEM = pl.BlockSpec(memory_space=pltpu.SMEM)
NT = (((1,), (1,)), ((), ()))
NN = (((1,), (0,)), ((), ()))
TN = (((0,), (0,)), ((), ()))


def dot(a, b, dims):
    return lax.dot_general(a, b, dims, preferred_element_type=jnp.float32)


def swaps_along(size):
    return [
        [(p, p + 1) for p in range(first, size - 1, 2)] for first in (0, 1) if first + 1 < size
    ]


def both_ways(pairs):
    return [(a, b) for a, b in pairs] + [(b, a) for a, b in pairs]


def row_route(swap, col_count):
    return [
        (a * col_count + col, b * col_count + col)
        for a, b in both_ways(swap)
        for col in range(col_count)
    ]


def col_route(swap, row_count, col_count):
    return [
        (row * col_count + a, row * col_count + b)
        for a, b in both_ways(swap)
        for row in range(row_count)
    ]


def partner(at, place, size):
    other = jnp.where(lax.rem(place, 2) == at, place + 1, place - 1)
    return jnp.clip(other, 0, size - 1), (other >= 0) & (other < size)


def table_rows(plan):
    cols = 1
    frames = cols + plan.nc
    flips = frames + plan.nf
    return cols, frames, flips


def table_shape(plan):
    rows = table_rows(plan)[-1] + plan.pairs
    return jax.ShapeDtypeStruct((-(-rows // 8) * 8, plan.hd), jnp.int32)


def prepare_kernel(plan, offsets_ref, counts_ref, q_ref, k_ref, v_ref, *refs):
    table_ref, plane_ref, across_ref, q_out_ref, sems = refs
    hd = plan.hd
    flips, copies = [], []
    for pair in range(plan.pairs):
        hits = jnp.int32(0)
        for slot in range(offsets_ref.shape[2]):
            hits = hits | jnp.abs(offsets_ref[2 * pair, 0, slot])
        flip = jnp.where(hits != 0, 1, 0).astype(jnp.int32)
        flips.append(flip)
        at = pl.ds(pair * hd, hd)
        for kind, near_ref in enumerate((plane_ref, across_ref)):
            head = 2 * pair + (flip if kind == 0 else 1 - flip)
            cols = pl.ds(pl.multiple_of(head * hd, hd), hd)
            targets = [
                (k_ref, near_ref.at[0, :, at]),
                (v_ref, near_ref.at[1, :, at]),
                (q_ref, q_out_ref.at[:, pl.ds((2 * pair + kind) * hd, hd)]),
            ]
            for source, target in targets:
                sem = sems.at[len(copies)]
                copies.append(pltpu.make_async_copy(source.at[:, cols], target, sem))
                copies[-1].start()
    frame, spot = lax.axis_index("frame"), lax.axis_index("tile")
    row, col = lax.div(spot, plan.col_count), lax.rem(spot, plan.col_count)
    entries = [counts_ref[frame, spot]]
    for at in range(plan.nc):
        other, there = partner(at, col, plan.col_count)
        entries.append(jnp.where(there, counts_ref[frame, row * plan.col_count + other], 0))
    for at in range(plan.nf):
        other, there = partner(at, frame, plan.frame_count)
        entries.append(jnp.where(there, counts_ref[other, spot], 0))
    entries += flips
    entries += [jnp.int32(0)] * (table_ref.shape[0] - len(entries))
    for at, entry in enumerate(entries):
        table_ref[at : at + 1, :] = jnp.full((1, hd), entry, jnp.int32)
    for copy in copies:
        copy.wait()


def gather_kernel(plan, table_ref, grad_ref, *refs):
    got_refs, out_ref = refs[:-1], refs[-1]
    section = lax.axis_index("section")
    sections = len(refs)
    flips = table_rows(plan)[-1]
    count = table_ref[0:1, :]
    rows, width, hd = grad_ref.shape[0], out_ref.shape[1], plan.hd
    at_rows = lax.broadcasted_iota(jnp.int32, (rows, hd), 0)
    for k in range(sections):
        holder = lax.rem(section + sections - k, sections)
        live = at_rows + holder * rows < count
        start = pl.multiple_of(holder * rows, rows)
        for pair in range(plan.pairs):
            heads = []
            for head in (2 * pair, 2 * pair + 1):
                at = pl.multiple_of(section * width + head * hd, hd)
                if k == 0:
                    part = grad_ref[:, pl.ds(at, hd)]
                else:
                    part = got_refs[k - 1][:, pl.ds(at, hd)]
                heads.append(jnp.where(live, part.astype(jnp.float32), 0.0))
            for i, part in enumerate(in_order(table_ref, flips + pair, *heads)):
                part = part.astype(out_ref.dtype)
                out_ref[pl.ds(start, rows), pl.ds((2 * pair + i) * hd, hd)] = part


def in_order(table_ref, row, a, b):
    flip = jnp.broadcast_to(table_ref[row : row + 1, :], a.shape) != 0
    return jnp.where(flip, b, a), jnp.where(flip, a, b)


def windows(plan, kv_refs):
    cols, frames, _ = table_rows(plan)
    per_kind = (kv_refs[: 1 + plan.nc], kv_refs[1 + plan.nc :])
    block = 0
    for pair in range(plan.pairs):
        for kind, first in ((0, cols), (1, frames)):
            slots = []
            for at, ref in enumerate(per_kind[kind]):
                row = 0 if at == 0 else first + at - 1
                slots.append((block, ref, pl.ds(pair * plan.hd, plan.hd), row))
                block += 1
            yield pair, kind, pl.ds((2 * pair + kind) * plan.hd, plan.hd), slots


def block_count(plan):
    return plan.pairs * (2 + plan.nc + plan.nf)


def block_weights(plan, table_ref, ref, at, row, q):
    at_rows = lax.broadcasted_iota(jnp.int32, (plan.tile, plan.hd), 0)
    bias = jnp.where(at_rows < table_ref[row : row + 1, :], 0.0, DEAD)
    bias = jnp.concatenate([bias] * (plan.tile // plan.hd), axis=1)
    scores = dot(ref[0, :, at], q, NT) * plan.factor + bias
    top = jnp.max(scores, axis=0, keepdims=True)
    weight = jnp.exp2(scores - top)
    return weight, top, jnp.sum(weight, axis=0, keepdims=True)


def merge(parts):
    top = functools.reduce(jnp.maximum, [log_total for log_total, _ in parts])
    weights = [jnp.exp2(log_total - top) for log_total, _ in parts]
    total = sum(weights)
    mean = sum(w * mean for w, (_, mean) in zip(weights, parts)) / total
    return top + jnp.log(total) * LOG2E, mean


def totals_at(plan, at, pair, kind):
    return pl.ds(4 * at + 2 * kind, 2), pl.ds(pair * plan.tile, plan.tile)


def totals_shape(plan, sets):
    return jax.ShapeDtypeStruct((4 * sets, plan.pairs * plan.tile), jnp.float32)


def totals(parts):
    top = functools.reduce(jnp.maximum, [top for top, _, _ in parts])
    weights = [jnp.exp2(part_top - top) for part_top, _, _ in parts]
    total = sum(w * total for w, (_, total, _) in zip(weights, parts))
    cross = sum(w * cross for w, (_, _, cross) in zip(weights, parts))
    return jnp.concatenate([top + jnp.log(total) * LOG2E, cross / total], axis=0)


def own_kernel(plan, table_ref, q_ref, grad_ref, *refs):
    *kv_refs, weight_ref, top_ref, slope_ref, total_ref = refs
    for pair, kind, cols, slots in windows(plan, kv_refs):
        parts = []
        for block, ref, at, row in slots:
            weight, top, total = block_weights(plan, table_ref, ref, at, row, q_ref[:, cols])
            slope = dot(ref[1, :, at], grad_ref[:, cols], NT)
            weight_ref[block] = weight
            slope_ref[block] = slope
            top_ref[block : block + 1, :] = top
            parts.append((top, total, jnp.sum(weight * slope, axis=0, keepdims=True)))
        total_ref[totals_at(plan, 0, pair, kind)] = totals(parts)


def order_kernel(plan, table_ref, q_ref, out_ref):
    hd = plan.hd
    flips = table_rows(plan)[-1]
    for pair in range(plan.pairs):
        cols = [pl.ds((2 * pair + i) * hd, hd) for i in (0, 1)]
        heads = [q_ref[:, at].astype(jnp.float32) for at in cols]
        for at, part in zip(cols, in_order(table_ref, flips + pair, *heads)):
            out_ref[:, at] = part.astype(out_ref.dtype)


def far_weights_kernel(plan, table_ref, q_ref, *refs):
    *kv_refs, weight_ref, top_ref, sum_ref = refs
    for pair, kind, cols, slots in windows(plan, kv_refs):
        for block, ref, at, row in slots:
            weight, top, total = block_weights(plan, table_ref, ref, at, row, q_ref[:, cols])
            weight_ref[block] = weight
            top_ref[block : block + 1, :] = top
            sum_ref[block : block + 1, :] = total


def far_totals_kernel(plan, weight_ref, top_ref, sum_ref, own_ref, grad_ref, *refs):
    *kv_refs, slope_ref, total_ref = refs
    total_ref[0:4, :] = own_ref[...]
    for pair, kind, cols, slots in windows(plan, kv_refs):
        parts = []
        for block, ref, at, _ in slots:
            slope = dot(ref[1, :, at], grad_ref[:, cols], NT)
            slope_ref[block] = slope
            cross = jnp.sum(weight_ref[block] * slope, axis=0, keepdims=True)
            parts.append((top_ref[block : block + 1, :], sum_ref[block : block + 1, :], cross))
        total_ref[totals_at(plan, 1, pair, kind)] = totals(parts)


def add(total, term):
    return term if total is None else total + term


def far_sums_kernel(plan, weight_ref, top_ref, slope_ref, total_ref, *refs):
    *kv_refs, grad_ref, key_ref = refs
    for pair, kind, cols, slots in windows(plan, kv_refs):
        totals = total_ref[totals_at(plan, 1, pair, kind)]
        log_total, row_dot = totals[0:1], totals[1:2]
        grad_sum, key_sum = None, None
        for block, ref, at, _ in slots:
            softmax = weight_ref[block] * jnp.exp2(top_ref[block : block + 1, :] - log_total)
            grad_scores = softmax * (slope_ref[block] - row_dot)
            key = ref[0, :, at]
            grad_sum = add(grad_sum, dot(key, grad_scores.astype(jnp.bfloat16), TN))
            key_sum = add(key_sum, dot(key, softmax.astype(jnp.bfloat16), TN))
        grad_ref[cols, :] = grad_sum
        key_ref[cols, :] = key_sum


def far_queries_kernel(plan, *refs):
    refs = list(refs)
    take = lambda n: [refs.pop(0) for _ in range(n)]
    total_refs = take(plan.n_totals)
    sets = [take(3) for _ in range(plan.nr)]
    for place, (local_ref, grad_ref, key_ref) in enumerate(sets):
        for pair in range(plan.pairs):
            for kind in (0, 1):
                cols = pl.ds((2 * pair + kind) * plan.hd, plan.hd)
                log_total, row_dot = all_totals(plan, total_refs, 1 + place, pair, kind)
                local = local_ref[totals_at(plan, 1, pair, kind)]
                share = jnp.exp2(local[0:1] - log_total) * plan.scale
                total = grad_ref[cols, :] + (local[1:2] - row_dot) * key_ref[cols, :]
                refs[place][:, cols] = jnp.transpose(total * share).astype(refs[place].dtype)


def all_totals(plan, total_refs, place, pair, kind):
    parts = []
    for ref, at in plan.totals_of[place]:
        part = total_refs[ref][totals_at(plan, at, pair, kind)]
        parts.append((part[0:1], part[1:2]))
    return merge(parts)


def head_grads(plan, sets, total_refs, kv_refs):
    for pair, kind, cols, slots in windows(plan, kv_refs):
        totals = [all_totals(plan, total_refs, at, pair, kind) for at in range(len(sets))]
        log_totals, row_dots = zip(*totals)

        def tile_grads(block, places, log_totals=log_totals, row_dots=row_dots):
            softmax, grad_scores = [], []
            for place in places:
                weight_ref, top_ref, slope_ref, _, _ = sets[place]
                scale = jnp.exp2(top_ref[block : block + 1, :] - log_totals[place])
                part = weight_ref[block] * scale
                softmax.append(part.astype(jnp.bfloat16))
                part = part * (slope_ref[block] - row_dots[place])
                grad_scores.append(part.astype(jnp.bfloat16))
            return jnp.concatenate(softmax, axis=1), jnp.concatenate(grad_scores, axis=1)

        q = jnp.concatenate([q_ref[:, cols] for _, _, _, q_ref, _ in sets], axis=0)
        grad = jnp.concatenate([grad_ref[:, cols] for _, _, _, _, grad_ref in sets], axis=0)
        yield kind, cols, q, grad, slots, tile_grads


def first_grads_kernel(plan, *refs):
    refs = list(refs)
    take = lambda n: [refs.pop(0) for _ in range(n)]
    sets = [take(5) for _ in range(1 + plan.nr)]
    kv_refs, total_refs = take(2 + plan.nc + plan.nf), take(plan.n_totals)
    for kind, cols, q, grad, slots, tile_grads in head_grads(plan, sets, total_refs, kv_refs):
        if kind == 1:
            continue
        for (block, _, at, _), out_ref in zip(slots[1:], refs):
            softmax, grad_scores = tile_grads(block, range(1 + plan.nr))
            dk = dot(grad_scores, q, NN) * plan.scale
            out_ref[0, :, at] = dk.astype(jnp.bfloat16)
            out_ref[1, :, at] = dot(softmax, grad, NN).astype(jnp.bfloat16)


def last_grads_kernel(plan, *refs):
    refs = list(refs)
    take = lambda n: [refs.pop(0) for _ in range(n)]
    sets = [take(5) for _ in range(1 + plan.nr)]
    kv_refs, total_refs = take(2 + plan.nc + plan.nf), take(plan.n_totals)
    dq_ref, *own_refs = take(3)
    tile = plan.tile
    everyone, own = range(1 + plan.nr), range(1)
    for kind, cols, q, grad, slots, tile_grads in head_grads(plan, sets, total_refs, kv_refs):
        query_grad = None
        for slot, (block, ref, at, _) in enumerate(slots):
            near = kind == 0 and slot > 0
            softmax, grad_scores = tile_grads(block, own if near else everyone)
            query_grad = add(query_grad, dot(ref[0, :, at], grad_scores[:, :tile], TN))
            if near:
                continue
            dk = dot(grad_scores, q, NN) * plan.scale
            dv = dot(softmax, grad, NN)
            for i, out in enumerate((dk, dv)):
                if slot == 0:
                    own_refs[i][:, cols] = out
                else:
                    refs[slot - 1][i, :, at] = out.astype(jnp.bfloat16)
        dq_ref[:, cols] = jnp.transpose(query_grad * plan.scale)


def add_query_kernel(plan, table_ref, *refs):
    *refs, out_ref = refs
    flips, hd = table_rows(plan)[-1], plan.hd
    for pair in range(plan.pairs):
        cols = [pl.ds((2 * pair + kind) * hd, hd) for kind in (0, 1)]
        parts = [sum(ref[:, at].astype(jnp.float32) for ref in refs) for at in cols]
        for at, head in zip(cols, in_order(table_ref, flips + pair, *parts)):
            out_ref[:, at] = head.astype(out_ref.dtype)


def add_key_kernel(plan, table_ref, *refs):
    refs = list(refs)
    take = lambda n: [refs.pop(0) for _ in range(n)]
    flips, hd = table_rows(plan)[-1], plan.hd
    own, near = take(2), (take(plan.nc), take(plan.nf))
    for pair in range(plan.pairs):
        cols = [pl.ds((2 * pair + kind) * hd, hd) for kind in (0, 1)]
        near_at = pl.ds(pair * hd, hd)
        for i, out_ref in enumerate(refs):
            parts = []
            for kind in (0, 1):
                total = own[i][:, cols[kind]]
                for ref in near[kind]:
                    total = total + ref[i, :, near_at].astype(jnp.float32)
                parts.append(total)
            for at, head in zip(cols, in_order(table_ref, flips + pair, *parts)):
                out_ref[:, at] = head.astype(out_ref.dtype)


class Plan:
    pass


def params():
    return pltpu.CompilerParams(vmem_limit_bytes=VMEM_LIMIT)


def local(queries, key_rows, value_rows, grad_rows, offsets, counts):
    q, k, v, grad = queries[0, 0], key_rows[0, 0], value_rows[0, 0], grad_rows[0, 0]
    tile, width = q.shape
    heads = offsets.shape[0]
    pairs = heads // 2
    hd = width // heads
    sections = lax.axis_size("section")
    frame_count = lax.axis_size("frame")
    col_count = NCT
    row_count = lax.axis_size("tile") // col_count

    plan = Plan()
    plan.tile, plan.hd, plan.col_count = tile, hd, col_count
    plan.scale = 1.0 / math.sqrt(hd)
    plan.factor = plan.scale * LOG2E
    row_swaps = swaps_along(row_count)
    col_swaps = swaps_along(col_count)
    frame_swaps = swaps_along(frame_count)
    plan.nr, plan.nc, plan.nf = len(row_swaps), len(col_swaps), len(frame_swaps)
    plan.frame_count = frame_count
    row_routes = [row_route(swap, col_count) for swap in row_swaps]
    col_routes = [col_route(swap, row_count, col_count) for swap in col_swaps]
    frame_routes = [both_ways(swap) for swap in frame_swaps]

    def from_rows(x):
        return [lax.ppermute(x, "tile", route) for route in row_routes]

    vm = pl.BlockSpec(memory_space=pltpu.VMEM)
    plan.row_count = row_count

    plan.pairs = pairs

    def call(kernel, name, out_shape, flops, *operands, nbytes=BYTES):
        return pl.pallas_call(
            functools.partial(kernel, plan),
            out_shape=out_shape,
            in_specs=[vm] * len(operands),
            out_specs=[vm] * len(out_shape),
            compiler_params=params(),
            cost_estimate=pl.CostEstimate(
                flops=flops, bytes_accessed=nbytes, transcendentals=0
            ),
            name=name,
        )(*operands)

    low = jax.ShapeDtypeStruct((tile, width), jnp.bfloat16)
    wide = jax.ShapeDtypeStruct((tile, width), jnp.float32)
    packed = jax.ShapeDtypeStruct((2, tile, pairs * hd), jnp.bfloat16)
    blocks = block_count(plan)
    block_shape = jax.ShapeDtypeStruct((blocks, tile, tile), jnp.float32)
    rows_shape = jax.ShapeDtypeStruct((-(-blocks // 8) * 8, tile), jnp.float32)

    got = []
    for shift in range(1, sections):
        route = [(i, (i + shift) % sections) for i in range(sections)]
        got.append(lax.ppermute(grad, "section", route))
    far_q_raw = from_rows(q)

    hbm = pl.BlockSpec(memory_space=pl.ANY)
    table, plane_kv, across_kv, own_q = pl.pallas_call(
        functools.partial(prepare_kernel, plan),
        out_shape=[table_shape(plan), packed, packed, low],
        in_specs=[SMEM] * 2 + [hbm] * 3,
        out_specs=[vm] * 4,
        scratch_shapes=[pltpu.SemaphoreType.DMA((6 * pairs,))],
        compiler_params=pltpu.CompilerParams(vmem_limit_bytes=PREPARE_VMEM_LIMIT),
        cost_estimate=pl.CostEstimate(flops=0, bytes_accessed=0, transcendentals=0),
        name="prepare",
    )(jnp.transpose(offsets, (0, 2, 1)), counts, q, k, v)

    (own_grad,) = call(gather_kernel, "gather_grad", [low], 0, table, grad, *got)

    near_plane = [lax.ppermute(plane_kv, "tile", route) for route in col_routes]
    near_across = [lax.ppermute(across_kv, "frame", route) for route in frame_routes]
    kv = [plane_kv, *near_plane, across_kv, *near_across]
    far_grad = from_rows(own_grad)

    matmul = 2 * blocks * tile * tile * hd
    far_q = [call(order_kernel, "order_queries", [low], 0, table, raw)[0] for raw in far_q_raw]
    table, *far_q = lax.optimization_barrier((table, *far_q))
    own_weight, own_top, own_slope, own_total = call(
        own_kernel,
        "own_rows",
        [block_shape, rows_shape, block_shape, totals_shape(plan, 1)],
        2 * matmul,
        *(table, own_q, own_grad, *kv),
    )
    sets = [(own_weight, own_top, own_slope, own_q, own_grad)]
    far_totals = []
    for queries, far in zip(far_q, far_grad):
        weight, top, total = call(
            far_weights_kernel,
            "far_weights",
            [block_shape, rows_shape, rows_shape],
            matmul,
            *(table, queries, *kv),
        )
        slope, total = call(
            far_totals_kernel,
            "far_totals",
            [block_shape, totals_shape(plan, 2)],
            matmul,
            *(weight, top, total, own_total, far, *kv),
        )
        sets.append((weight, top, slope, queries, far))
        far_totals.append(total)
    shared, plan.totals_of = share_totals(own_total, far_totals, row_routes)
    plan.n_totals = len(shared)

    nq = 1 + plan.nr
    operands = [ref for refs in sets for ref in refs] + kv + shared
    parts = []
    for (weight, top, slope, _, _), total in zip(sets[1:], far_totals):
        sums = call(
            far_sums_kernel,
            "far_sums",
            [jax.ShapeDtypeStruct((width, tile), jnp.float32)] * 2,
            2 * matmul,
            *(weight, top, slope, total, *kv),
        )
        parts.append((total, *sums))
    far_dq = call(
        far_queries_kernel,
        "far_queries",
        [low] * plan.nr,
        0,
        *(*shared, *(ref for part in parts for ref in part)),
    )
    plane_out = call(
        first_grads_kernel, "first_grads", [packed] * plan.nc, nq * matmul, *operands
    )
    ready = lax.optimization_barrier((*far_dq, *plane_out))
    far_dq, plane_out = ready[: plan.nr], ready[plan.nr :]
    back = [lax.ppermute(x, "tile", r) for x, r in zip(far_dq, row_routes)]
    back_plane = [lax.ppermute(x, "tile", r) for x, r in zip(plane_out, col_routes)]
    own_dq, own_dk, own_dv, *across_out = call(
        last_grads_kernel,
        "last_grads",
        [wide] * 3 + [packed] * plan.nf,
        nq * matmul,
        *operands,
    )
    back_across = [lax.ppermute(x, "frame", r) for x, r in zip(across_out, frame_routes)]
    (dq,) = call(add_query_kernel, "add_query", [low], 0, table, own_dq, *back)
    dk, dv = call(
        add_key_kernel,
        "add_key",
        [low] * 2,
        0,
        *(table, own_dk, own_dv, *back_plane, *back_across),
    )
    return dq[None, None], dk[None, None], dv[None, None]


def share_totals(own, far, row_routes):
    if len(far) == 0:
        return [own], [[(0, 0)]]
    if len(far) == 1:
        back = lax.ppermute(far[0], "tile", row_routes[0])
        return [far[0], back], [[(0, 0), (1, 1)], [(0, 1), (1, 0)]]
    terms = [own]
    for part, route in zip(far, row_routes):
        term = lax.ppermute(part[4:], "tile", route)
        there = lax.ppermute(jnp.ones((8, 128), jnp.float32), "tile", route)[0, 0] > 0
        logs = jnp.array([1, 0, 1, 0], jnp.float32)[:, None]
        terms.append(jnp.where(there, term, DEAD * logs))
    merged = []
    for kind in (0, 1):
        merged += merge([(t[2 * kind], t[2 * kind + 1]) for t in terms])
    total = jnp.stack(merged)
    shared = [total] + [lax.ppermute(total, "tile", route) for route in row_routes]
    return shared, [[(at, 0)] for at in range(len(shared))]


def solution(mesh):
    return jax.shard_map(
        local,
        mesh=mesh,
        in_specs=(
            P("frame", "tile", None, "section"),
            P("frame", "tile", None, "section"),
            P("frame", "tile", None, "section"),
            P("frame", "tile", "section", None),
            P("section", None, None),
            P(),
        ),
        out_specs=(
            P("frame", "tile", None, "section"),
            P("frame", "tile", None, "section"),
            P("frame", "tile", None, "section"),
        ),
        check_vma=False,
    )
```

```python
import functools
import math

import jax
import jax.numpy as jnp
from jax import lax
from jax.experimental import pallas as pl
from jax.experimental.pallas import tpu as pltpu
from jax.sharding import PartitionSpec as P

NCT = 4
LOG2E = 1.4426950408889634
DEAD = -1e30
BYTES = 1 << 20
VMEM_LIMIT = 24 << 20
PREPARE_VMEM_LIMIT = 56 << 20

SMEM = pl.BlockSpec(memory_space=pltpu.SMEM)
NT = (((1,), (1,)), ((), ()))
NN = (((1,), (0,)), ((), ()))
TN = (((0,), (0,)), ((), ()))


def dot(a, b, dims):
    return lax.dot_general(a, b, dims, preferred_element_type=jnp.float32)


def swaps_along(size):
    return [
        [(p, p + 1) for p in range(first, size - 1, 2)] for first in (0, 1) if first + 1 < size
    ]


def both_ways(pairs):
    return [(a, b) for a, b in pairs] + [(b, a) for a, b in pairs]


def row_route(swap, col_count):
    return [
        (a * col_count + col, b * col_count + col)
        for a, b in both_ways(swap)
        for col in range(col_count)
    ]


def col_route(swap, row_count, col_count):
    return [
        (row * col_count + a, row * col_count + b)
        for a, b in both_ways(swap)
        for row in range(row_count)
    ]


def partner(at, place, size):
    other = jnp.where(lax.rem(place, 2) == at, place + 1, place - 1)
    return jnp.clip(other, 0, size - 1), (other >= 0) & (other < size)


def table_rows(plan):
    cols = 1
    frames = cols + plan.nc
    flips = frames + plan.nf
    return cols, frames, flips


def table_shape(plan):
    rows = table_rows(plan)[-1] + plan.pairs
    return jax.ShapeDtypeStruct((-(-rows // 8) * 8, plan.hd), jnp.int32)


def prepare_kernel(plan, offsets_ref, counts_ref, q_ref, k_ref, v_ref, *refs):
    table_ref, plane_ref, across_ref, q_out_ref, sems = refs
    hd = plan.hd
    flips, copies = [], []
    for pair in range(plan.pairs):
        hits = jnp.int32(0)
        for slot in range(offsets_ref.shape[2]):
            hits = hits | jnp.abs(offsets_ref[2 * pair, 0, slot])
        flip = jnp.where(hits != 0, 1, 0).astype(jnp.int32)
        flips.append(flip)
        at = pl.ds(pair * hd, hd)
        for kind, near_ref in enumerate((plane_ref, across_ref)):
            head = 2 * pair + (flip if kind == 0 else 1 - flip)
            cols = pl.ds(pl.multiple_of(head * hd, hd), hd)
            targets = [
                (k_ref, near_ref.at[0, :, at]),
                (v_ref, near_ref.at[1, :, at]),
                (q_ref, q_out_ref.at[:, pl.ds((2 * pair + kind) * hd, hd)]),
            ]
            for source, target in targets:
                sem = sems.at[len(copies)]
                copies.append(pltpu.make_async_copy(source.at[:, cols], target, sem))
                copies[-1].start()
    frame, spot = lax.axis_index("frame"), lax.axis_index("tile")
    row, col = lax.div(spot, plan.col_count), lax.rem(spot, plan.col_count)
    entries = [counts_ref[frame, spot]]
    for at in range(plan.nc):
        other, there = partner(at, col, plan.col_count)
        entries.append(jnp.where(there, counts_ref[frame, row * plan.col_count + other], 0))
    for at in range(plan.nf):
        other, there = partner(at, frame, plan.frame_count)
        entries.append(jnp.where(there, counts_ref[other, spot], 0))
    entries += flips
    entries += [jnp.int32(0)] * (table_ref.shape[0] - len(entries))
    for at, entry in enumerate(entries):
        table_ref[at : at + 1, :] = jnp.full((1, hd), entry, jnp.int32)
    for copy in copies:
        copy.wait()


def gather_kernel(plan, table_ref, grad_ref, *refs):
    got_refs, out_ref = refs[:-1], refs[-1]
    section = lax.axis_index("section")
    sections = len(refs)
    flips = table_rows(plan)[-1]
    count = table_ref[0:1, :]
    rows, width, hd = grad_ref.shape[0], out_ref.shape[1], plan.hd
    at_rows = lax.broadcasted_iota(jnp.int32, (rows, hd), 0)
    for k in range(sections):
        holder = lax.rem(section + sections - k, sections)
        live = at_rows + holder * rows < count
        start = pl.multiple_of(holder * rows, rows)
        for pair in range(plan.pairs):
            heads = []
            for head in (2 * pair, 2 * pair + 1):
                at = pl.multiple_of(section * width + head * hd, hd)
                if k == 0:
                    part = grad_ref[:, pl.ds(at, hd)]
                else:
                    part = got_refs[k - 1][:, pl.ds(at, hd)]
                heads.append(jnp.where(live, part.astype(jnp.float32), 0.0))
            for i, part in enumerate(in_order(table_ref, flips + pair, *heads)):
                part = part.astype(out_ref.dtype)
                out_ref[pl.ds(start, rows), pl.ds((2 * pair + i) * hd, hd)] = part


def in_order(table_ref, row, a, b):
    flip = jnp.broadcast_to(table_ref[row : row + 1, :], a.shape) != 0
    return jnp.where(flip, b, a), jnp.where(flip, a, b)


def windows(plan, kv_refs):
    cols, frames, _ = table_rows(plan)
    per_kind = (kv_refs[: 1 + plan.nc], kv_refs[1 + plan.nc :])
    block = 0
    for pair in range(plan.pairs):
        for kind, first in ((0, cols), (1, frames)):
            slots = []
            for at, ref in enumerate(per_kind[kind]):
                row = 0 if at == 0 else first + at - 1
                slots.append((block, ref, pl.ds(pair * plan.hd, plan.hd), row))
                block += 1
            yield pair, kind, pl.ds((2 * pair + kind) * plan.hd, plan.hd), slots


def block_count(plan):
    return plan.pairs * (2 + plan.nc + plan.nf)


def block_weights(plan, table_ref, ref, at, row, q):
    at_rows = lax.broadcasted_iota(jnp.int32, (plan.tile, plan.hd), 0)
    bias = jnp.where(at_rows < table_ref[row : row + 1, :], 0.0, DEAD)
    bias = jnp.concatenate([bias] * (plan.tile // plan.hd), axis=1)
    scores = dot(ref[0, :, at], q, NT) * plan.factor + bias
    top = jnp.max(scores, axis=0, keepdims=True)
    weight = jnp.exp2(scores - top)
    return weight, top, jnp.sum(weight, axis=0, keepdims=True)


def merge(parts):
    top = functools.reduce(jnp.maximum, [log_total for log_total, _ in parts])
    weights = [jnp.exp2(log_total - top) for log_total, _ in parts]
    total = sum(weights)
    mean = sum(w * mean for w, (_, mean) in zip(weights, parts)) / total
    return top + jnp.log(total) * LOG2E, mean


def totals_at(plan, at, pair, kind):
    return pl.ds(4 * at + 2 * kind, 2), pl.ds(pair * plan.tile, plan.tile)


def totals_shape(plan, sets):
    return jax.ShapeDtypeStruct((4 * sets, plan.pairs * plan.tile), jnp.float32)


def totals(parts):
    top = functools.reduce(jnp.maximum, [top for top, _, _ in parts])
    weights = [jnp.exp2(part_top - top) for part_top, _, _ in parts]
    total = sum(w * total for w, (_, total, _) in zip(weights, parts))
    cross = sum(w * cross for w, (_, _, cross) in zip(weights, parts))
    return jnp.concatenate([top + jnp.log(total) * LOG2E, cross / total], axis=0)


def own_kernel(plan, table_ref, q_ref, grad_ref, *refs):
    *kv_refs, weight_ref, top_ref, slope_ref, total_ref = refs
    for pair, kind, cols, slots in windows(plan, kv_refs):
        parts = []
        for block, ref, at, row in slots:
            weight, top, total = block_weights(plan, table_ref, ref, at, row, q_ref[:, cols])
            slope = dot(ref[1, :, at], grad_ref[:, cols], NT)
            weight_ref[block] = weight
            slope_ref[block] = slope
            top_ref[block : block + 1, :] = top
            parts.append((top, total, jnp.sum(weight * slope, axis=0, keepdims=True)))
        total_ref[totals_at(plan, 0, pair, kind)] = totals(parts)


def order_kernel(plan, table_ref, q_ref, out_ref):
    hd = plan.hd
    flips = table_rows(plan)[-1]
    for pair in range(plan.pairs):
        cols = [pl.ds((2 * pair + i) * hd, hd) for i in (0, 1)]
        heads = [q_ref[:, at].astype(jnp.float32) for at in cols]
        for at, part in zip(cols, in_order(table_ref, flips + pair, *heads)):
            out_ref[:, at] = part.astype(out_ref.dtype)


def far_weights_kernel(plan, table_ref, q_ref, *refs):
    *kv_refs, weight_ref, top_ref, sum_ref = refs
    for pair, kind, cols, slots in windows(plan, kv_refs):
        for block, ref, at, row in slots:
            weight, top, total = block_weights(plan, table_ref, ref, at, row, q_ref[:, cols])
            weight_ref[block] = weight
            top_ref[block : block + 1, :] = top
            sum_ref[block : block + 1, :] = total


def far_values_kernel(plan, weight_ref, top_ref, sum_ref, *refs):
    *kv_refs, log_ref, mean_ref = refs
    for pair, kind, cols, slots in windows(plan, kv_refs):
        tops = [top_ref[block : block + 1, :] for block, _, _, _ in slots]
        top = functools.reduce(jnp.maximum, tops)
        total, low_total, values = None, None, None
        for slot_top, (block, ref, at, _) in zip(tops, slots):
            scale = jnp.exp2(slot_top - top)
            low = weight_ref[block].astype(jnp.bfloat16)
            low_sum = jnp.sum(low.astype(jnp.float32), axis=0, keepdims=True)
            total = add(total, scale * sum_ref[block : block + 1, :])
            low_total = add(low_total, scale * low_sum)
            values = add(values, scale * dot(ref[1, :, at], low, TN))
        log_total = top + jnp.log(total) * LOG2E
        log_ref[totals_at(plan, 0, pair, kind)] = jnp.concatenate([log_total] * 2, axis=0)
        mean_ref[cols, :] = values / low_total


def far_totals_kernel(plan, log_ref, mean_ref, own_ref, grad_ref, total_ref):
    total_ref[0:4, :] = own_ref[...]
    for pair in range(plan.pairs):
        for kind in (0, 1):
            cols = pl.ds((2 * pair + kind) * plan.hd, plan.hd)
            grad = jnp.transpose(grad_ref[:, cols].astype(jnp.float32))
            row_dot = jnp.sum(mean_ref[cols, :] * grad, axis=0, keepdims=True)
            log_total = log_ref[totals_at(plan, 0, pair, kind)][0:1]
            total = jnp.concatenate([log_total, row_dot], axis=0)
            total_ref[totals_at(plan, 1, pair, kind)] = total


def far_slopes_kernel(plan, grad_ref, *refs):
    *kv_refs, slope_ref = refs
    for _, _, cols, slots in windows(plan, kv_refs):
        for block, ref, at, _ in slots:
            slope_ref[block] = dot(ref[1, :, at], grad_ref[:, cols], NT)


def add(total, term):
    return term if total is None else total + term


def far_sums_kernel(plan, weight_ref, top_ref, slope_ref, total_ref, *refs):
    *kv_refs, grad_ref, key_ref = refs
    for pair, kind, cols, slots in windows(plan, kv_refs):
        totals = total_ref[totals_at(plan, 1, pair, kind)]
        log_total, row_dot = totals[0:1], totals[1:2]
        grad_sum, key_sum = None, None
        for block, ref, at, _ in slots:
            softmax = weight_ref[block] * jnp.exp2(top_ref[block : block + 1, :] - log_total)
            grad_scores = softmax * (slope_ref[block] - row_dot)
            key = ref[0, :, at]
            grad_sum = add(grad_sum, dot(key, grad_scores.astype(jnp.bfloat16), TN))
            key_sum = add(key_sum, dot(key, softmax.astype(jnp.bfloat16), TN))
        grad_ref[cols, :] = grad_sum
        key_ref[cols, :] = key_sum


def far_queries_kernel(plan, *refs):
    refs = list(refs)
    take = lambda n: [refs.pop(0) for _ in range(n)]
    total_refs = take(plan.n_totals)
    sets = [take(3) for _ in range(plan.nr)]
    for place, (local_ref, grad_ref, key_ref) in enumerate(sets):
        for pair in range(plan.pairs):
            for kind in (0, 1):
                cols = pl.ds((2 * pair + kind) * plan.hd, plan.hd)
                log_total, row_dot = all_totals(plan, total_refs, 1 + place, pair, kind)
                local = local_ref[totals_at(plan, 1, pair, kind)]
                share = jnp.exp2(local[0:1] - log_total) * plan.scale
                total = grad_ref[cols, :] + (local[1:2] - row_dot) * key_ref[cols, :]
                refs[place][:, cols] = jnp.transpose(total * share).astype(refs[place].dtype)


def all_totals(plan, total_refs, place, pair, kind):
    parts = []
    for ref, at in plan.totals_of[place]:
        part = total_refs[ref][totals_at(plan, at, pair, kind)]
        parts.append((part[0:1], part[1:2]))
    return merge(parts)


def head_grads(plan, sets, total_refs, kv_refs):
    for pair, kind, cols, slots in windows(plan, kv_refs):
        totals = [all_totals(plan, total_refs, at, pair, kind) for at in range(len(sets))]
        log_totals, row_dots = zip(*totals)

        def tile_grads(block, places, log_totals=log_totals, row_dots=row_dots):
            softmax, grad_scores = [], []
            for place in places:
                weight_ref, top_ref, slope_ref, _, _ = sets[place]
                scale = jnp.exp2(top_ref[block : block + 1, :] - log_totals[place])
                part = weight_ref[block] * scale
                softmax.append(part.astype(jnp.bfloat16))
                part = part * (slope_ref[block] - row_dots[place])
                grad_scores.append(part.astype(jnp.bfloat16))
            return jnp.concatenate(softmax, axis=1), jnp.concatenate(grad_scores, axis=1)

        q = jnp.concatenate([q_ref[:, cols] for _, _, _, q_ref, _ in sets], axis=0)
        grad = jnp.concatenate([grad_ref[:, cols] for _, _, _, _, grad_ref in sets], axis=0)
        yield kind, cols, q, grad, slots, tile_grads


def first_grads_kernel(plan, *refs):
    refs = list(refs)
    take = lambda n: [refs.pop(0) for _ in range(n)]
    sets = [take(5) for _ in range(1 + plan.nr)]
    kv_refs, total_refs = take(2 + plan.nc + plan.nf), take(plan.n_totals)
    for kind, cols, q, grad, slots, tile_grads in head_grads(plan, sets, total_refs, kv_refs):
        if kind == 1:
            continue
        for (block, _, at, _), out_ref in zip(slots[1:], refs):
            softmax, grad_scores = tile_grads(block, range(1 + plan.nr))
            dk = dot(grad_scores, q, NN) * plan.scale
            out_ref[0, :, at] = dk.astype(jnp.bfloat16)
            out_ref[1, :, at] = dot(softmax, grad, NN).astype(jnp.bfloat16)


def last_grads_kernel(plan, *refs):
    refs = list(refs)
    take = lambda n: [refs.pop(0) for _ in range(n)]
    sets = [take(5) for _ in range(1 + plan.nr)]
    kv_refs, total_refs = take(2 + plan.nc + plan.nf), take(plan.n_totals)
    dq_ref, *own_refs = take(3)
    tile = plan.tile
    everyone, own = range(1 + plan.nr), range(1)
    for kind, cols, q, grad, slots, tile_grads in head_grads(plan, sets, total_refs, kv_refs):
        query_grad = None
        for slot, (block, ref, at, _) in enumerate(slots):
            near = kind == 0 and slot > 0
            softmax, grad_scores = tile_grads(block, own if near else everyone)
            query_grad = add(query_grad, dot(ref[0, :, at], grad_scores[:, :tile], TN))
            if near:
                continue
            dk = dot(grad_scores, q, NN) * plan.scale
            dv = dot(softmax, grad, NN)
            for i, out in enumerate((dk, dv)):
                if slot == 0:
                    own_refs[i][:, cols] = out
                else:
                    refs[slot - 1][i, :, at] = out.astype(jnp.bfloat16)
        dq_ref[:, cols] = jnp.transpose(query_grad * plan.scale)


def add_query_kernel(plan, table_ref, *refs):
    *refs, out_ref = refs
    flips, hd = table_rows(plan)[-1], plan.hd
    for pair in range(plan.pairs):
        cols = [pl.ds((2 * pair + kind) * hd, hd) for kind in (0, 1)]
        parts = [sum(ref[:, at].astype(jnp.float32) for ref in refs) for at in cols]
        for at, head in zip(cols, in_order(table_ref, flips + pair, *parts)):
            out_ref[:, at] = head.astype(out_ref.dtype)


def add_key_kernel(plan, table_ref, *refs):
    refs = list(refs)
    take = lambda n: [refs.pop(0) for _ in range(n)]
    flips, hd = table_rows(plan)[-1], plan.hd
    own, near = take(2), (take(plan.nc), take(plan.nf))
    out_refs, (buffer, sems) = take(2), refs
    copies = []
    for pair in range(plan.pairs):
        cols = [pl.ds((2 * pair + kind) * hd, hd) for kind in (0, 1)]
        near_at = pl.ds(pair * hd, hd)
        for i, out_ref in enumerate(out_refs):
            parts = []
            for kind in (0, 1):
                total = own[i][:, cols[kind]]
                for ref in near[kind]:
                    total = total + ref[i, :, near_at].astype(jnp.float32)
                parts.append(total)
            for at, head in zip(cols, in_order(table_ref, flips + pair, *parts)):
                buffer[i, :, at] = head.astype(buffer.dtype)
            whole = pl.ds(2 * pair * hd, 2 * hd)
            sem = sems.at[len(copies)]
            copies.append(pltpu.make_async_copy(buffer.at[i, :, whole], out_ref.at[:, whole], sem))
            copies[-1].start()
    for copy in copies:
        copy.wait()


class Plan:
    pass


def params():
    return pltpu.CompilerParams(vmem_limit_bytes=VMEM_LIMIT)


def local(queries, key_rows, value_rows, grad_rows, offsets, counts):
    q, k, v, grad = queries[0, 0], key_rows[0, 0], value_rows[0, 0], grad_rows[0, 0]
    tile, width = q.shape
    heads = offsets.shape[0]
    pairs = heads // 2
    hd = width // heads
    sections = lax.axis_size("section")
    frame_count = lax.axis_size("frame")
    col_count = NCT
    row_count = lax.axis_size("tile") // col_count

    plan = Plan()
    plan.tile, plan.hd, plan.col_count = tile, hd, col_count
    plan.scale = 1.0 / math.sqrt(hd)
    plan.factor = plan.scale * LOG2E
    row_swaps = swaps_along(row_count)
    col_swaps = swaps_along(col_count)
    frame_swaps = swaps_along(frame_count)
    plan.nr, plan.nc, plan.nf = len(row_swaps), len(col_swaps), len(frame_swaps)
    plan.frame_count = frame_count
    row_routes = [row_route(swap, col_count) for swap in row_swaps]
    col_routes = [col_route(swap, row_count, col_count) for swap in col_swaps]
    frame_routes = [both_ways(swap) for swap in frame_swaps]

    def from_rows(x):
        return [lax.ppermute(x, "tile", route) for route in row_routes]

    vm = pl.BlockSpec(memory_space=pltpu.VMEM)
    plan.row_count = row_count

    plan.pairs = pairs

    def call(kernel, name, out_shape, flops, *operands, nbytes=BYTES):
        return pl.pallas_call(
            functools.partial(kernel, plan),
            out_shape=out_shape,
            in_specs=[vm] * len(operands),
            out_specs=[vm] * len(out_shape),
            compiler_params=params(),
            cost_estimate=pl.CostEstimate(
                flops=flops, bytes_accessed=nbytes, transcendentals=0
            ),
            name=name,
        )(*operands)

    low = jax.ShapeDtypeStruct((tile, width), jnp.bfloat16)
    wide = jax.ShapeDtypeStruct((tile, width), jnp.float32)
    packed = jax.ShapeDtypeStruct((2, tile, pairs * hd), jnp.bfloat16)
    wide_turned = jax.ShapeDtypeStruct((width, tile), jnp.float32)
    blocks = block_count(plan)
    block_shape = jax.ShapeDtypeStruct((blocks, tile, tile), jnp.float32)
    rows_shape = jax.ShapeDtypeStruct((-(-blocks // 8) * 8, tile), jnp.float32)

    got = []
    for shift in range(1, sections):
        route = [(i, (i + shift) % sections) for i in range(sections)]
        got.append(lax.ppermute(grad, "section", route))
    far_q_raw = from_rows(q)

    hbm = pl.BlockSpec(memory_space=pl.ANY)
    table, plane_kv, across_kv, own_q = pl.pallas_call(
        functools.partial(prepare_kernel, plan),
        out_shape=[table_shape(plan), packed, packed, low],
        in_specs=[SMEM] * 2 + [hbm] * 3,
        out_specs=[vm] * 4,
        scratch_shapes=[pltpu.SemaphoreType.DMA((6 * pairs,))],
        compiler_params=pltpu.CompilerParams(vmem_limit_bytes=PREPARE_VMEM_LIMIT),
        cost_estimate=pl.CostEstimate(flops=0, bytes_accessed=0, transcendentals=0),
        name="prepare",
    )(jnp.transpose(offsets, (0, 2, 1)), counts, q, k, v)

    (own_grad,) = call(gather_kernel, "gather_grad", [low], 0, table, grad, *got)

    near_plane = [lax.ppermute(plane_kv, "tile", route) for route in col_routes]
    near_across = [lax.ppermute(across_kv, "frame", route) for route in frame_routes]
    kv = [plane_kv, *near_plane, across_kv, *near_across]
    far_grad = from_rows(own_grad)

    matmul = 2 * blocks * tile * tile * hd
    far_q = [call(order_kernel, "order_queries", [low], 0, table, raw)[0] for raw in far_q_raw]
    table, *far_q = lax.optimization_barrier((table, *far_q))
    own_weight, own_top, own_slope, own_total = call(
        own_kernel,
        "own_rows",
        [block_shape, rows_shape, block_shape, totals_shape(plan, 1)],
        2 * matmul,
        *(table, own_q, own_grad, *kv),
    )
    sets = [(own_weight, own_top, own_slope, own_q, own_grad)]
    far_totals = []
    for queries, far in zip(far_q, far_grad):
        weight, top, total = call(
            far_weights_kernel,
            "far_weights",
            [block_shape, rows_shape, rows_shape],
            matmul,
            *(table, queries, *kv),
        )
        log_total, mean = call(
            far_values_kernel,
            "far_values",
            [totals_shape(plan, 1), wide_turned],
            matmul,
            *(weight, top, total, *kv),
        )
        (total,) = call(
            far_totals_kernel,
            "far_totals",
            [totals_shape(plan, 2)],
            0,
            *(log_total, mean, own_total, far),
        )
        far, _ = lax.optimization_barrier((far, total))
        (slope,) = call(far_slopes_kernel, "far_slopes", [block_shape], matmul, far, *kv)
        sets.append((weight, top, slope, queries, far))
        far_totals.append(total)
    shared, plan.totals_of = share_totals(own_total, far_totals, row_routes)
    plan.n_totals = len(shared)

    nq = 1 + plan.nr
    operands = [ref for refs in sets for ref in refs] + kv + shared
    parts = []
    for (weight, top, slope, _, _), total in zip(sets[1:], far_totals):
        sums = call(
            far_sums_kernel,
            "far_sums",
            [wide_turned] * 2,
            2 * matmul,
            *(weight, top, slope, total, *kv),
        )
        parts.append((total, *sums))
    far_dq = call(
        far_queries_kernel,
        "far_queries",
        [low] * plan.nr,
        0,
        *(*shared, *(ref for part in parts for ref in part)),
    )
    plane_out = call(
        first_grads_kernel, "first_grads", [packed] * plan.nc, nq * matmul, *operands
    )
    ready = lax.optimization_barrier((*far_dq, *plane_out))
    far_dq, plane_out = ready[: plan.nr], ready[plan.nr :]
    back = [lax.ppermute(x, "tile", r) for x, r in zip(far_dq, row_routes)]
    back_plane = [lax.ppermute(x, "tile", r) for x, r in zip(plane_out, col_routes)]
    own_dq, own_dk, own_dv, *across_out = call(
        last_grads_kernel,
        "last_grads",
        [wide] * 3 + [packed] * plan.nf,
        nq * matmul,
        *operands,
    )
    back_across = [lax.ppermute(x, "frame", r) for x, r in zip(across_out, frame_routes)]
    (dq,) = call(add_query_kernel, "add_query", [low], 0, table, own_dq, *back)
    operands = [table, own_dk, own_dv, *back_plane, *back_across]
    dk, dv = pl.pallas_call(
        functools.partial(add_key_kernel, plan),
        out_shape=[low] * 2,
        in_specs=[vm] * len(operands),
        out_specs=[hbm] * 2,
        scratch_shapes=[
            pltpu.VMEM((2, tile, width), jnp.bfloat16),
            pltpu.SemaphoreType.DMA((2 * pairs,)),
        ],
        compiler_params=params(),
        cost_estimate=pl.CostEstimate(flops=0, bytes_accessed=BYTES, transcendentals=0),
        name="add_key",
    )(*operands)
    return dq[None, None], dk[None, None], dv[None, None]


def share_totals(own, far, row_routes):
    if len(far) == 0:
        return [own], [[(0, 0)]]
    if len(far) == 1:
        back = lax.ppermute(far[0], "tile", row_routes[0])
        return [far[0], back], [[(0, 0), (1, 1)], [(0, 1), (1, 0)]]
    terms = [own]
    for part, route in zip(far, row_routes):
        term = lax.ppermute(part[4:], "tile", route)
        there = lax.ppermute(jnp.ones((8, 128), jnp.float32), "tile", route)[0, 0] > 0
        logs = jnp.array([1, 0, 1, 0], jnp.float32)[:, None]
        terms.append(jnp.where(there, term, DEAD * logs))
    merged = []
    for kind in (0, 1):
        merged += merge([(t[2 * kind], t[2 * kind + 1]) for t in terms])
    total = jnp.stack(merged)
    shared = [total] + [lax.ppermute(total, "tile", route) for route in row_routes]
    return shared, [[(at, 0)] for at in range(len(shared))]


def solution(mesh):
    return jax.shard_map(
        local,
        mesh=mesh,
        in_specs=(
            P("frame", "tile", None, "section"),
            P("frame", "tile", None, "section"),
            P("frame", "tile", None, "section"),
            P("frame", "tile", "section", None),
            P("section", None, None),
            P(),
        ),
        out_specs=(
            P("frame", "tile", None, "section"),
            P("frame", "tile", None, "section"),
            P("frame", "tile", None, "section"),
        ),
        check_vma=False,
    )
```

```python
import functools
import math

import jax
import jax.numpy as jnp
from jax import lax
from jax.experimental import pallas as pl
from jax.experimental.pallas import tpu as pltpu
from jax.sharding import PartitionSpec as P

NCT = 4
LOG2E = 1.4426950408889634
DEAD = -1e30
BYTES = 1 << 20
VMEM_LIMIT = 24 << 20
PREPARE_VMEM_LIMIT = 56 << 20

SMEM = pl.BlockSpec(memory_space=pltpu.SMEM)
NT = (((1,), (1,)), ((), ()))
NN = (((1,), (0,)), ((), ()))
TN = (((0,), (0,)), ((), ()))


def dot(a, b, dims):
    return lax.dot_general(a, b, dims, preferred_element_type=jnp.float32)


def swaps_along(size):
    return [
        [(p, p + 1) for p in range(first, size - 1, 2)] for first in (0, 1) if first + 1 < size
    ]


def both_ways(pairs):
    return [(a, b) for a, b in pairs] + [(b, a) for a, b in pairs]


def row_route(swap, col_count):
    return [
        (a * col_count + col, b * col_count + col)
        for a, b in both_ways(swap)
        for col in range(col_count)
    ]


def col_route(swap, row_count, col_count):
    return [
        (row * col_count + a, row * col_count + b)
        for a, b in both_ways(swap)
        for row in range(row_count)
    ]


def partner(at, place, size):
    other = jnp.where(lax.rem(place, 2) == at, place + 1, place - 1)
    return jnp.clip(other, 0, size - 1), (other >= 0) & (other < size)


def table_rows(plan):
    cols = 1
    frames = cols + plan.nc
    flips = frames + plan.nf
    return cols, frames, flips


def table_shape(plan):
    rows = table_rows(plan)[-1] + plan.pairs
    return jax.ShapeDtypeStruct((-(-rows // 8) * 8, plan.hd), jnp.int32)


def prepare_kernel(plan, offsets_ref, counts_ref, q_ref, k_ref, v_ref, *refs):
    table_ref, plane_ref, across_ref, q_out_ref, sems = refs
    hd = plan.hd
    flips, copies = [], []
    for pair in range(plan.pairs):
        hits = jnp.int32(0)
        for slot in range(offsets_ref.shape[2]):
            hits = hits | jnp.abs(offsets_ref[2 * pair, 0, slot])
        flip = jnp.where(hits != 0, 1, 0).astype(jnp.int32)
        flips.append(flip)
        at = pl.ds(pair * hd, hd)
        for kind, near_ref in enumerate((plane_ref, across_ref)):
            head = 2 * pair + (flip if kind == 0 else 1 - flip)
            cols = pl.ds(pl.multiple_of(head * hd, hd), hd)
            targets = [
                (k_ref, near_ref.at[0, :, at]),
                (v_ref, near_ref.at[1, :, at]),
                (q_ref, q_out_ref.at[:, pl.ds((2 * pair + kind) * hd, hd)]),
            ]
            for source, target in targets:
                sem = sems.at[len(copies)]
                copies.append(pltpu.make_async_copy(source.at[:, cols], target, sem))
                copies[-1].start()
    frame, spot = lax.axis_index("frame"), lax.axis_index("tile")
    row, col = lax.div(spot, plan.col_count), lax.rem(spot, plan.col_count)
    entries = [counts_ref[frame, spot]]
    for at in range(plan.nc):
        other, there = partner(at, col, plan.col_count)
        entries.append(jnp.where(there, counts_ref[frame, row * plan.col_count + other], 0))
    for at in range(plan.nf):
        other, there = partner(at, frame, plan.frame_count)
        entries.append(jnp.where(there, counts_ref[other, spot], 0))
    entries += flips
    entries += [jnp.int32(0)] * (table_ref.shape[0] - len(entries))
    for at, entry in enumerate(entries):
        table_ref[at : at + 1, :] = jnp.full((1, hd), entry, jnp.int32)
    for copy in copies:
        copy.wait()


def gather_kernel(plan, table_ref, grad_ref, *refs):
    got_refs, out_ref = refs[:-1], refs[-1]
    section = lax.axis_index("section")
    sections = len(refs)
    flips = table_rows(plan)[-1]
    count = table_ref[0:1, :]
    rows, width, hd = grad_ref.shape[0], out_ref.shape[1], plan.hd
    at_rows = lax.broadcasted_iota(jnp.int32, (rows, hd), 0)
    for k in range(sections):
        holder = lax.rem(section + sections - k, sections)
        live = at_rows + holder * rows < count
        start = pl.multiple_of(holder * rows, rows)
        for pair in range(plan.pairs):
            heads = []
            for head in (2 * pair, 2 * pair + 1):
                at = pl.multiple_of(section * width + head * hd, hd)
                if k == 0:
                    part = grad_ref[:, pl.ds(at, hd)]
                else:
                    part = got_refs[k - 1][:, pl.ds(at, hd)]
                heads.append(jnp.where(live, part.astype(jnp.float32), 0.0))
            for i, part in enumerate(in_order(table_ref, flips + pair, *heads)):
                part = part.astype(out_ref.dtype)
                out_ref[pl.ds(start, rows), pl.ds((2 * pair + i) * hd, hd)] = part


def in_order(table_ref, row, a, b):
    flip = jnp.broadcast_to(table_ref[row : row + 1, :], a.shape) != 0
    return jnp.where(flip, b, a), jnp.where(flip, a, b)


def windows(plan, kv_refs):
    cols, frames, _ = table_rows(plan)
    per_kind = (kv_refs[: 1 + plan.nc], kv_refs[1 + plan.nc :])
    block = 0
    for pair in range(plan.pairs):
        for kind, first in ((0, cols), (1, frames)):
            slots = []
            for at, ref in enumerate(per_kind[kind]):
                row = 0 if at == 0 else first + at - 1
                slots.append((block, ref, pl.ds(pair * plan.hd, plan.hd), row))
                block += 1
            yield pair, kind, pl.ds((2 * pair + kind) * plan.hd, plan.hd), slots


def block_count(plan):
    return plan.pairs * (2 + plan.nc + plan.nf)


def block_weights(plan, table_ref, ref, at, row, q):
    at_rows = lax.broadcasted_iota(jnp.int32, (plan.tile, plan.hd), 0)
    bias = jnp.where(at_rows < table_ref[row : row + 1, :], 0.0, DEAD)
    bias = jnp.concatenate([bias] * (plan.tile // plan.hd), axis=1)
    scores = dot(ref[0, :, at], q, NT) * plan.factor + bias
    top = jnp.max(scores, axis=0, keepdims=True)
    weight = jnp.exp2(scores - top)
    return weight, top, jnp.sum(weight, axis=0, keepdims=True)


def merge(parts):
    top = functools.reduce(jnp.maximum, [log_total for log_total, _ in parts])
    weights = [jnp.exp2(log_total - top) for log_total, _ in parts]
    total = sum(weights)
    mean = sum(w * mean for w, (_, mean) in zip(weights, parts)) / total
    return top + jnp.log(total) * LOG2E, mean


def totals_at(plan, at, pair, kind):
    return pl.ds(4 * at + 2 * kind, 2), pl.ds(pair * plan.tile, plan.tile)


def totals_shape(plan, sets):
    return jax.ShapeDtypeStruct((4 * sets, plan.pairs * plan.tile), jnp.float32)


def totals(parts):
    top = functools.reduce(jnp.maximum, [top for top, _, _ in parts])
    weights = [jnp.exp2(part_top - top) for part_top, _, _ in parts]
    total = sum(w * total for w, (_, total, _) in zip(weights, parts))
    cross = sum(w * cross for w, (_, _, cross) in zip(weights, parts))
    return jnp.concatenate([top + jnp.log(total) * LOG2E, cross / total], axis=0)


def own_kernel(plan, table_ref, q_ref, grad_ref, *refs):
    *kv_refs, weight_ref, top_ref, slope_ref, total_ref = refs
    for pair, kind, cols, slots in windows(plan, kv_refs):
        parts = []
        for block, ref, at, row in slots:
            weight, top, total = block_weights(plan, table_ref, ref, at, row, q_ref[:, cols])
            slope = dot(ref[1, :, at], grad_ref[:, cols], NT)
            weight_ref[block] = weight
            slope_ref[block] = slope
            top_ref[block : block + 1, :] = top
            parts.append((top, total, jnp.sum(weight * slope, axis=0, keepdims=True)))
        total_ref[totals_at(plan, 0, pair, kind)] = totals(parts)


def order_kernel(plan, table_ref, q_ref, out_ref):
    hd = plan.hd
    flips = table_rows(plan)[-1]
    for pair in range(plan.pairs):
        cols = [pl.ds((2 * pair + i) * hd, hd) for i in (0, 1)]
        heads = [q_ref[:, at].astype(jnp.float32) for at in cols]
        for at, part in zip(cols, in_order(table_ref, flips + pair, *heads)):
            out_ref[:, at] = part.astype(out_ref.dtype)


def far_weights_kernel(plan, table_ref, q_ref, *refs):
    *kv_refs, weight_ref, top_ref, sum_ref = refs
    for pair, kind, cols, slots in windows(plan, kv_refs):
        for block, ref, at, row in slots:
            weight, top, total = block_weights(plan, table_ref, ref, at, row, q_ref[:, cols])
            weight_ref[block] = weight
            top_ref[block : block + 1, :] = top
            sum_ref[block : block + 1, :] = total


def far_values_kernel(plan, weight_ref, top_ref, sum_ref, *refs):
    *kv_refs, log_ref, mean_ref = refs
    for pair, kind, cols, slots in windows(plan, kv_refs):
        tops = [top_ref[block : block + 1, :] for block, _, _, _ in slots]
        top = functools.reduce(jnp.maximum, tops)
        total, low_total, values = None, None, None
        for slot_top, (block, ref, at, _) in zip(tops, slots):
            scale = jnp.exp2(slot_top - top)
            low = weight_ref[block].astype(jnp.bfloat16)
            low_sum = jnp.sum(low.astype(jnp.float32), axis=0, keepdims=True)
            total = add(total, scale * sum_ref[block : block + 1, :])
            low_total = add(low_total, scale * low_sum)
            values = add(values, scale * dot(ref[1, :, at], low, TN))
        log_total = top + jnp.log(total) * LOG2E
        log_ref[totals_at(plan, 0, pair, kind)] = jnp.concatenate([log_total] * 2, axis=0)
        mean_ref[cols, :] = values / low_total


def far_totals_kernel(plan, log_ref, mean_ref, own_ref, grad_ref, total_ref):
    total_ref[0:4, :] = own_ref[...]
    for pair in range(plan.pairs):
        for kind in (0, 1):
            cols = pl.ds((2 * pair + kind) * plan.hd, plan.hd)
            grad = jnp.transpose(grad_ref[:, cols].astype(jnp.float32))
            row_dot = jnp.sum(mean_ref[cols, :] * grad, axis=0, keepdims=True)
            log_total = log_ref[totals_at(plan, 0, pair, kind)][0:1]
            total = jnp.concatenate([log_total, row_dot], axis=0)
            total_ref[totals_at(plan, 1, pair, kind)] = total


def far_slopes_kernel(plan, grad_ref, *refs):
    *kv_refs, slope_ref = refs
    for _, _, cols, slots in windows(plan, kv_refs):
        for block, ref, at, _ in slots:
            slope_ref[block] = dot(ref[1, :, at], grad_ref[:, cols], NT)


def add(total, term):
    return term if total is None else total + term


def far_sums_kernel(plan, weight_ref, top_ref, slope_ref, total_ref, *refs):
    *kv_refs, grad_ref, key_ref = refs
    for pair, kind, cols, slots in windows(plan, kv_refs):
        totals = total_ref[totals_at(plan, 1, pair, kind)]
        log_total, row_dot = totals[0:1], totals[1:2]
        grad_sum, key_sum = None, None
        for block, ref, at, _ in slots:
            softmax = weight_ref[block] * jnp.exp2(top_ref[block : block + 1, :] - log_total)
            grad_scores = softmax * (slope_ref[block] - row_dot)
            key = ref[0, :, at]
            grad_sum = add(grad_sum, dot(key, grad_scores.astype(jnp.bfloat16), TN))
            key_sum = add(key_sum, dot(key, softmax.astype(jnp.bfloat16), TN))
        grad_ref[cols, :] = grad_sum
        key_ref[cols, :] = key_sum


def far_queries_kernel(plan, *refs):
    refs = list(refs)
    take = lambda n: [refs.pop(0) for _ in range(n)]
    total_refs = take(plan.n_totals)
    sets = [take(3) for _ in range(plan.nr)]
    for place, (local_ref, grad_ref, key_ref) in enumerate(sets):
        for pair in range(plan.pairs):
            for kind in (0, 1):
                cols = pl.ds((2 * pair + kind) * plan.hd, plan.hd)
                log_total, row_dot = all_totals(plan, total_refs, 1 + place, pair, kind)
                local = local_ref[totals_at(plan, 1, pair, kind)]
                share = jnp.exp2(local[0:1] - log_total) * plan.scale
                total = grad_ref[cols, :] + (local[1:2] - row_dot) * key_ref[cols, :]
                refs[place][:, cols] = jnp.transpose(total * share).astype(refs[place].dtype)


def all_totals(plan, total_refs, place, pair, kind):
    parts = []
    for ref, at in plan.totals_of[place]:
        part = total_refs[ref][totals_at(plan, at, pair, kind)]
        parts.append((part[0:1], part[1:2]))
    return merge(parts)


def head_grads(plan, sets, total_refs, kv_refs):
    for pair, kind, cols, slots in windows(plan, kv_refs):
        totals = [all_totals(plan, total_refs, at, pair, kind) for at in range(len(sets))]
        log_totals, row_dots = zip(*totals)

        def tile_grads(block, places, log_totals=log_totals, row_dots=row_dots):
            softmax, grad_scores = [], []
            for place in places:
                weight_ref, top_ref, slope_ref, _, _ = sets[place]
                scale = jnp.exp2(top_ref[block : block + 1, :] - log_totals[place])
                part = weight_ref[block] * scale
                softmax.append(part.astype(jnp.bfloat16))
                part = part * (slope_ref[block] - row_dots[place])
                grad_scores.append(part.astype(jnp.bfloat16))
            return jnp.concatenate(softmax, axis=1), jnp.concatenate(grad_scores, axis=1)

        q = jnp.concatenate([q_ref[:, cols] for _, _, _, q_ref, _ in sets], axis=0)
        grad = jnp.concatenate([grad_ref[:, cols] for _, _, _, _, grad_ref in sets], axis=0)
        yield kind, cols, q, grad, slots, tile_grads


def first_grads_kernel(plan, *refs):
    refs = list(refs)
    take = lambda n: [refs.pop(0) for _ in range(n)]
    sets = [take(5) for _ in range(1 + plan.nr)]
    kv_refs, total_refs = take(2 + plan.nc + plan.nf), take(plan.n_totals)
    for kind, cols, q, grad, slots, tile_grads in head_grads(plan, sets, total_refs, kv_refs):
        if kind == 1:
            continue
        for (block, _, at, _), out_ref in zip(slots[1:], refs):
            softmax, grad_scores = tile_grads(block, range(1 + plan.nr))
            dk = dot(grad_scores, q, NN) * plan.scale
            out_ref[0, :, at] = dk.astype(jnp.bfloat16)
            out_ref[1, :, at] = dot(softmax, grad, NN).astype(jnp.bfloat16)


def send_kernel(plan, *refs, split):
    refs, plane_refs = refs[: len(refs) - plan.nc], refs[len(refs) - plan.nc :]
    refs, dq_refs = refs[: len(refs) - plan.nr], refs[len(refs) - plan.nr :]
    far_queries_kernel(plan, *refs[:split], *dq_refs)
    first_grads_kernel(plan, *refs[split:], *plane_refs)


def last_grads_kernel(plan, *refs):
    refs = list(refs)
    take = lambda n: [refs.pop(0) for _ in range(n)]
    sets = [take(5) for _ in range(1 + plan.nr)]
    kv_refs, total_refs = take(2 + plan.nc + plan.nf), take(plan.n_totals)
    dq_ref, *own_refs = take(3)
    tile = plan.tile
    everyone, own = range(1 + plan.nr), range(1)
    for kind, cols, q, grad, slots, tile_grads in head_grads(plan, sets, total_refs, kv_refs):
        query_grad = None
        for slot, (block, ref, at, _) in enumerate(slots):
            near = kind == 0 and slot > 0
            softmax, grad_scores = tile_grads(block, own if near else everyone)
            query_grad = add(query_grad, dot(ref[0, :, at], grad_scores[:, :tile], TN))
            if near:
                continue
            dk = dot(grad_scores, q, NN) * plan.scale
            dv = dot(softmax, grad, NN)
            for i, out in enumerate((dk, dv)):
                if slot == 0:
                    own_refs[i][:, cols] = out
                else:
                    refs[slot - 1][i, :, at] = out.astype(jnp.bfloat16)
        dq_ref[:, cols] = jnp.transpose(query_grad * plan.scale)


def add_query_kernel(plan, table_ref, *refs):
    *refs, out_ref = refs
    flips, hd = table_rows(plan)[-1], plan.hd
    for pair in range(plan.pairs):
        cols = [pl.ds((2 * pair + kind) * hd, hd) for kind in (0, 1)]
        parts = [sum(ref[:, at].astype(jnp.float32) for ref in refs) for at in cols]
        for at, head in zip(cols, in_order(table_ref, flips + pair, *parts)):
            out_ref[:, at] = head.astype(out_ref.dtype)


def add_key_kernel(plan, table_ref, *refs):
    refs = list(refs)
    take = lambda n: [refs.pop(0) for _ in range(n)]
    flips, hd = table_rows(plan)[-1], plan.hd
    own, near = take(2), (take(plan.nc), take(plan.nf))
    out_refs, (buffer, sems) = take(2), refs
    copies = []
    for pair in range(plan.pairs):
        cols = [pl.ds((2 * pair + kind) * hd, hd) for kind in (0, 1)]
        near_at = pl.ds(pair * hd, hd)
        for i, out_ref in enumerate(out_refs):
            parts = []
            for kind in (0, 1):
                total = own[i][:, cols[kind]]
                for ref in near[kind]:
                    total = total + ref[i, :, near_at].astype(jnp.float32)
                parts.append(total)
            for at, head in zip(cols, in_order(table_ref, flips + pair, *parts)):
                buffer[i, :, at] = head.astype(buffer.dtype)
            whole = pl.ds(2 * pair * hd, 2 * hd)
            sem = sems.at[len(copies)]
            copies.append(pltpu.make_async_copy(buffer.at[i, :, whole], out_ref.at[:, whole], sem))
            copies[-1].start()
    for copy in copies:
        copy.wait()


class Plan:
    pass


def params():
    return pltpu.CompilerParams(vmem_limit_bytes=VMEM_LIMIT)


def local(queries, key_rows, value_rows, grad_rows, offsets, counts):
    q, k, v, grad = queries[0, 0], key_rows[0, 0], value_rows[0, 0], grad_rows[0, 0]
    tile, width = q.shape
    heads = offsets.shape[0]
    pairs = heads // 2
    hd = width // heads
    sections = lax.axis_size("section")
    frame_count = lax.axis_size("frame")
    col_count = NCT
    row_count = lax.axis_size("tile") // col_count

    plan = Plan()
    plan.tile, plan.hd, plan.col_count = tile, hd, col_count
    plan.scale = 1.0 / math.sqrt(hd)
    plan.factor = plan.scale * LOG2E
    row_swaps = swaps_along(row_count)
    col_swaps = swaps_along(col_count)
    frame_swaps = swaps_along(frame_count)
    plan.nr, plan.nc, plan.nf = len(row_swaps), len(col_swaps), len(frame_swaps)
    plan.frame_count = frame_count
    row_routes = [row_route(swap, col_count) for swap in row_swaps]
    col_routes = [col_route(swap, row_count, col_count) for swap in col_swaps]
    frame_routes = [both_ways(swap) for swap in frame_swaps]

    def from_rows(x):
        return [lax.ppermute(x, "tile", route) for route in row_routes]

    vm = pl.BlockSpec(memory_space=pltpu.VMEM)
    plan.row_count = row_count

    plan.pairs = pairs

    def call(kernel, name, out_shape, flops, *operands, nbytes=BYTES):
        return pl.pallas_call(
            functools.partial(kernel, plan),
            out_shape=out_shape,
            in_specs=[vm] * len(operands),
            out_specs=[vm] * len(out_shape),
            compiler_params=params(),
            cost_estimate=pl.CostEstimate(
                flops=flops, bytes_accessed=nbytes, transcendentals=0
            ),
            name=name,
        )(*operands)

    low = jax.ShapeDtypeStruct((tile, width), jnp.bfloat16)
    wide = jax.ShapeDtypeStruct((tile, width), jnp.float32)
    packed = jax.ShapeDtypeStruct((2, tile, pairs * hd), jnp.bfloat16)
    wide_turned = jax.ShapeDtypeStruct((width, tile), jnp.float32)
    blocks = block_count(plan)
    block_shape = jax.ShapeDtypeStruct((blocks, tile, tile), jnp.float32)
    rows_shape = jax.ShapeDtypeStruct((-(-blocks // 8) * 8, tile), jnp.float32)

    got = []
    for shift in range(1, sections):
        route = [(i, (i + shift) % sections) for i in range(sections)]
        got.append(lax.ppermute(grad, "section", route))
    far_q_raw = from_rows(q)

    hbm = pl.BlockSpec(memory_space=pl.ANY)
    table, plane_kv, across_kv, own_q = pl.pallas_call(
        functools.partial(prepare_kernel, plan),
        out_shape=[table_shape(plan), packed, packed, low],
        in_specs=[SMEM] * 2 + [hbm] * 3,
        out_specs=[vm] * 4,
        scratch_shapes=[pltpu.SemaphoreType.DMA((6 * pairs,))],
        compiler_params=pltpu.CompilerParams(vmem_limit_bytes=PREPARE_VMEM_LIMIT),
        cost_estimate=pl.CostEstimate(flops=0, bytes_accessed=0, transcendentals=0),
        name="prepare",
    )(jnp.transpose(offsets, (0, 2, 1)), counts, q, k, v)

    (own_grad,) = call(gather_kernel, "gather_grad", [low], 0, table, grad, *got)

    near_plane = [lax.ppermute(plane_kv, "tile", route) for route in col_routes]
    near_across = [lax.ppermute(across_kv, "frame", route) for route in frame_routes]
    kv = [plane_kv, *near_plane, across_kv, *near_across]
    far_grad = from_rows(own_grad)

    matmul = 2 * blocks * tile * tile * hd
    far_q = [call(order_kernel, "order_queries", [low], 0, table, raw)[0] for raw in far_q_raw]
    table, *far_q = lax.optimization_barrier((table, *far_q))
    own_weight, own_top, own_slope, own_total = call(
        own_kernel,
        "own_rows",
        [block_shape, rows_shape, block_shape, totals_shape(plan, 1)],
        2 * matmul,
        *(table, own_q, own_grad, *kv),
    )
    sets = [(own_weight, own_top, own_slope, own_q, own_grad)]
    far_totals = []
    for queries, far in zip(far_q, far_grad):
        weight, top, total = call(
            far_weights_kernel,
            "far_weights",
            [block_shape, rows_shape, rows_shape],
            matmul,
            *(table, queries, *kv),
        )
        log_total, mean = call(
            far_values_kernel,
            "far_values",
            [totals_shape(plan, 1), wide_turned],
            matmul,
            *(weight, top, total, *kv),
        )
        (total,) = call(
            far_totals_kernel,
            "far_totals",
            [totals_shape(plan, 2)],
            0,
            *(log_total, mean, own_total, far),
        )
        far, _ = lax.optimization_barrier((far, total))
        (slope,) = call(far_slopes_kernel, "far_slopes", [block_shape], matmul, far, *kv)
        sets.append((weight, top, slope, queries, far))
        far_totals.append(total)
    shared, plan.totals_of = share_totals(own_total, far_totals, row_routes)
    plan.n_totals = len(shared)

    nq = 1 + plan.nr
    operands = [ref for refs in sets for ref in refs] + kv + shared
    parts = []
    for (weight, top, slope, _, _), total in zip(sets[1:], far_totals):
        sums = call(
            far_sums_kernel,
            "far_sums",
            [wide_turned] * 2,
            2 * matmul,
            *(weight, top, slope, total, *kv),
        )
        parts.append((total, *sums))
    sums_operands = [*shared, *(ref for part in parts for ref in part)]
    outs = call(
        functools.partial(send_kernel, split=len(sums_operands)),
        "first_grads",
        [low] * plan.nr + [packed] * plan.nc,
        nq * matmul,
        *(*sums_operands, *operands),
    )
    far_dq, plane_out = outs[: plan.nr], outs[plan.nr :]
    back = [lax.ppermute(x, "tile", r) for x, r in zip(far_dq, row_routes)]
    back_plane = [lax.ppermute(x, "tile", r) for x, r in zip(plane_out, col_routes)]
    own_dq, own_dk, own_dv, *across_out = call(
        last_grads_kernel,
        "last_grads",
        [wide] * 3 + [packed] * plan.nf,
        nq * matmul,
        *operands,
    )
    back_across = [lax.ppermute(x, "frame", r) for x, r in zip(across_out, frame_routes)]
    (dq,) = call(add_query_kernel, "add_query", [low], 0, table, own_dq, *back)
    operands = [table, own_dk, own_dv, *back_plane, *back_across]
    dk, dv = pl.pallas_call(
        functools.partial(add_key_kernel, plan),
        out_shape=[low] * 2,
        in_specs=[vm] * len(operands),
        out_specs=[hbm] * 2,
        scratch_shapes=[
            pltpu.VMEM((2, tile, width), jnp.bfloat16),
            pltpu.SemaphoreType.DMA((2 * pairs,)),
        ],
        compiler_params=params(),
        cost_estimate=pl.CostEstimate(flops=0, bytes_accessed=BYTES, transcendentals=0),
        name="add_key",
    )(*operands)
    return dq[None, None], dk[None, None], dv[None, None]


def share_totals(own, far, row_routes):
    if len(far) == 0:
        return [own], [[(0, 0)]]
    if len(far) == 1:
        back = lax.ppermute(far[0], "tile", row_routes[0])
        return [far[0], back], [[(0, 0), (1, 1)], [(0, 1), (1, 0)]]
    terms = [own]
    for part, route in zip(far, row_routes):
        term = lax.ppermute(part[4:], "tile", route)
        there = lax.ppermute(jnp.ones((8, 128), jnp.float32), "tile", route)[0, 0] > 0
        logs = jnp.array([1, 0, 1, 0], jnp.float32)[:, None]
        terms.append(jnp.where(there, term, DEAD * logs))
    merged = []
    for kind in (0, 1):
        merged += merge([(t[2 * kind], t[2 * kind + 1]) for t in terms])
    total = jnp.stack(merged)
    shared = [total] + [lax.ppermute(total, "tile", route) for route in row_routes]
    return shared, [[(at, 0)] for at in range(len(shared))]


def solution(mesh):
    return jax.shard_map(
        local,
        mesh=mesh,
        in_specs=(
            P("frame", "tile", None, "section"),
            P("frame", "tile", None, "section"),
            P("frame", "tile", None, "section"),
            P("frame", "tile", "section", None),
            P("section", None, None),
            P(),
        ),
        out_specs=(
            P("frame", "tile", None, "section"),
            P("frame", "tile", None, "section"),
            P("frame", "tile", None, "section"),
        ),
        check_vma=False,
    )
```
